256 devices in a mesh: dp: 32 (over y, x, core), tensor: 8 (over z).
Axes of the slice: x: 4, y: 4, z: 8, core: 2. Of those that a mesh axis runs over, the one named last changes fastest.
Arguments:
- tokens: bfloat16 [8192, 4096], P(('dp', 'tensor')), may hold values from -6 to 6
- grad_out: bfloat16 [8192, 16384], P('dp', 'tensor'), may hold values from -0.0625 to 0.0625
- owner: int32 [8, 128], P('tensor'), may hold values from 0 to 31, as said below
- left_factor: float32 [8, 160, 256, 256], P('tensor', 'dp'), may hold values from -0.15 to 2, as said below
- right_factor: float32 [8, 160, 256, 256], P('tensor', 'dp'), may hold values from -0.15 to 2, as said below
- left_basis: bfloat16 [8, 160, 256, 256], P('tensor', 'dp'), may hold values from -0.375 to 0.375
- right_basis: bfloat16 [8, 160, 256, 256], P('tensor', 'dp'), may hold values from -0.375 to 0.375
- first_moment: bfloat16 [8, 160, 256, 256], P('tensor', 'dp'), may hold values from -0.29882812 to 0.29882812
- second_moment: bfloat16 [8, 160, 256, 256], P('tensor', 'dp'), may hold values from 0.0049743652 to 0.049804688
Outputs:
- update: bfloat16 [8, 128, 256, 256], P('tensor', 'dp')
- left_factor_new: float32 [8, 160, 256, 256], P('tensor', 'dp')
- right_factor_new: float32 [8, 160, 256, 256], P('tensor', 'dp')
- first_moment_new: bfloat16 [8, 160, 256, 256], P('tensor', 'dp')
- second_moment_new: bfloat16 [8, 160, 256, 256], P('tensor', 'dp')
The draws below stay inside these ranges and needn't reach their ends.
Inputs may be any that keep to these rules, and one draw needn't show every extreme that they name: For every t, each owner holds between 3 and 5 blocks, some owner exactly 5; among the blocks k with one value of k // 4, no owner holds more than 1, and some owner exactly 1. `left_factor`: each block is symmetric. `right_factor`: each block is symmetric.
All inputs are finite; a program needn't handle non-finite values.
Results may differ from the reference program's by a relative error of at most 0.035.
Values may be sent and summed in bfloat16 or wider, within the bound.
No kernel may reach another device: no remote copies, remote signals or barrier semaphores. Data moves between devices by JAX's collectives and lax.ppermute only.
A program may use at most 192 MiB of HBM per device.

```python
import math
import jax
import jax.numpy as jnp
from jax import lax

BLOCK = 256
D = 4096
FF = 16384
TOK_DEV = 256
TOKENS = 8192
ROW_BLOCKS = 16
COL_BLOCKS = 8
NBLK = 128
HOME = 4
SLOTS = 5
N_DP = 32
N_TENSOR = 8


def owner_grid(key):
    key_one, key_two, key_three, key_four = jax.random.split(key, 4)
    pair_count = N_DP // 2
    spread = jax.random.randint(key_one, (pair_count,), 0, HOME // 4 + 1)
    spread = jnp.where(jnp.arange(pair_count) == 0, HOME // 4, spread)
    counts = jnp.stack([HOME + spread, HOME - spread], axis=1).reshape(N_DP)
    bounds = jnp.cumsum(counts)
    positions = jnp.arange(NBLK)
    listed = jnp.sum((positions[:, None] >= bounds[None, :]).astype(jnp.int32), axis=1)
    relabel = jax.random.permutation(key_two, N_DP)
    listed = relabel[listed]
    layout_grid = listed.reshape(HOME, N_DP).T
    layout_grid = layout_grid[jax.random.permutation(key_three, N_DP)]
    layout_grid = layout_grid[:, jax.random.permutation(key_four, HOME)]
    return layout_grid.reshape(NBLK).astype(jnp.int32)


def draw_owner(key, part):
    key = jax.random.fold_in(key, 11)
    return jax.vmap(owner_grid)(jax.random.split(key, N_TENSOR))


def symmetric_blocks(key):
    key_one, key_two = jax.random.split(key)
    shape = (N_TENSOR, N_DP * SLOTS, BLOCK, BLOCK)
    noise = jax.random.uniform(key_one, shape, jnp.float32, -0.15, 0.15)
    mirror = 0.5 * (noise + jnp.swapaxes(noise, 2, 3))
    levels = jnp.exp(jax.random.uniform(key_two, shape[:3], jnp.float32, jnp.log(0.5), jnp.log(2.0)))
    diagonal = jnp.eye(BLOCK, dtype=jnp.float32)
    return mirror * (1.0 - diagonal) + diagonal * levels[..., None]


def draw_left_factor(key, part):
    key = jax.random.fold_in(key, 21)
    return symmetric_blocks(key)


def draw_right_factor(key, part):
    key = jax.random.fold_in(key, 22)
    return symmetric_blocks(key)


def shard_levels(stream_key, dims, cuts, low, largest):
    def one(position, shards_of):
        steps = jax.random.uniform(jax.random.fold_in(jax.random.fold_in(stream_key, 6), position), (shards_of,), jnp.float32, low / len(cuts), largest / len(cuts))
        return jnp.repeat(jnp.exp(steps), dims[position] // shards_of).reshape((-1,) + (1,) * (len(dims) - position - 1))

    loudness = one(*cuts[0])
    for cut in cuts[1:]:
        loudness = loudness * one(*cut)
    return loudness


def bell_draw(stream_key, extent, scale, reach, cuts=(), held_as=jnp.bfloat16):
    array = scale * jax.random.normal(stream_key, extent, jnp.float32)
    if cuts:
        array = array * shard_levels(stream_key, extent, cuts, -0.22, 0.18)
    return jnp.clip(array, -reach, reach).astype(held_as)


def setup_inputs(seed: int = 0) -> dict:
    streams_of = jax.random.split(jax.random.key(seed), 10)
    tokens = bell_draw(streams_of[0], (TOKENS, D), 1.0, 6.0, ((0, 256),))
    grad_out = bell_draw(streams_of[1], (TOKENS, FF), TOKENS ** -0.5, 0.0625, ((0, 32), (1, 8)))
    owner = draw_owner(jax.random.fold_in(streams_of[9], 71), 0)
    left_factor = draw_left_factor(jax.random.fold_in(streams_of[9], 71), 0)
    right_factor = draw_right_factor(jax.random.fold_in(streams_of[9], 71), 0)
    left_basis = bell_draw(streams_of[5], (N_TENSOR, N_DP * SLOTS, BLOCK, BLOCK), BLOCK ** -0.5, 0.375, ((0, 8), (1, 32)))
    right_basis = bell_draw(streams_of[6], (N_TENSOR, N_DP * SLOTS, BLOCK, BLOCK), BLOCK ** -0.5, 0.375, ((0, 8), (1, 32)))
    first_moment = bell_draw(streams_of[7], (N_TENSOR, N_DP * SLOTS, BLOCK, BLOCK), 0.05, 0.29882812, ((0, 8), (1, 32)))
    second_moment = jnp.clip(jnp.exp(math.log(0.049804688) - 2.3038113 * jax.random.uniform(streams_of[8], (N_TENSOR, N_DP * SLOTS, BLOCK, BLOCK), jnp.float32) ** shard_levels(streams_of[8], (N_TENSOR, N_DP * SLOTS, BLOCK, BLOCK), ((0, 8), (1, 32)), -0.2, 0.2)), 0.0049743652, 0.049804688).astype(jnp.bfloat16)
    return dict(tokens=tokens, grad_out=grad_out, owner=owner, left_factor=left_factor, right_factor=right_factor, left_basis=left_basis, right_basis=right_basis, first_moment=first_moment, second_moment=second_moment)


factor_decay = 0.9
first_decay = 0.95
second_decay = 0.95
epsilon_value = 1e-08

def rounded(value):
    return lax.optimization_barrier(value.astype(jnp.bfloat16)).astype(jnp.float32)

def slot_positions(owner_row):
    columns = jnp.arange(N_DP, dtype=jnp.int32)
    onehot = (owner_row[:, None] == columns[None, :]).astype(jnp.int32)
    before = jnp.cumsum(onehot, axis=0) - onehot
    rank = lax.optimization_barrier(jnp.sum(before * onehot, axis=1))
    return (owner_row * SLOTS + rank).astype(jnp.int32)

def shard_gradient(tokens, grad_cols):
    width = grad_cols.shape[1]
    token_parts = tokens.reshape(N_DP, TOK_DEV, D)
    grad_parts = grad_cols.reshape(N_DP, TOK_DEV, width)

    def add_part(total, pieces):
        partial_sum = jnp.dot(pieces[0].T, pieces[1], preferred_element_type=jnp.float32)
        return (total + rounded(partial_sum), None)
    start_total = jnp.zeros((D, width), jnp.float32)
    total, unused = lax.scan(add_part, start_total, (token_parts, grad_parts))
    blocks = total.reshape(ROW_BLOCKS, BLOCK, COL_BLOCKS, BLOCK).transpose(2, 0, 1, 3)
    return blocks.reshape(NBLK, BLOCK, BLOCK).astype(jnp.bfloat16)

def soap_blocks(grads, left, right, basis_left, basis_right, first, second):
    highest = lax.Precision.HIGHEST
    gradient = grads.astype(jnp.float32)
    rotate_left = basis_left.astype(jnp.float32)
    rotate_right = basis_right.astype(jnp.float32)
    gram_left = jnp.einsum('sik,sjk->sij', gradient, gradient, precision=highest)
    gram_right = jnp.einsum('ski,skj->sij', gradient, gradient, precision=highest)
    left_new = factor_decay * left + (1.0 - factor_decay) / BLOCK * gram_left
    right_new = factor_decay * right + (1.0 - factor_decay) / BLOCK * gram_right
    halfway = rounded(jnp.einsum('ski,skj->sij', rotate_left, gradient, precision=highest))
    rotated = jnp.einsum('sik,skj->sij', halfway, rotate_right, precision=highest)
    first_new = first_decay * first.astype(jnp.float32) + (1.0 - first_decay) * rotated
    second_new = second_decay * second.astype(jnp.float32) + (1.0 - second_decay) * rotated * rotated
    ratio = rounded(first_new / (jnp.sqrt(second_new) + epsilon_value))
    turned = rounded(jnp.einsum('sik,skj->sij', rotate_left, ratio, precision=highest))
    update = jnp.einsum('sik,sjk->sij', turned, rotate_right, precision=highest).astype(jnp.bfloat16)
    return (left_new, right_new, first_new.astype(jnp.bfloat16), second_new.astype(jnp.bfloat16), update)

def reference(tokens, grad_out, owner, left_factor, right_factor, left_basis, right_basis, first_moment, second_moment):
    columns = grad_out.shape[1] // N_TENSOR
    updates = []
    lefts = []
    rights = []
    firsts = []
    seconds = []
    for shard in range(N_TENSOR):
        grads = shard_gradient(tokens, grad_out[:, shard * columns:(shard + 1) * columns])
        places = slot_positions(owner[shard])
        results = soap_blocks(grads, left_factor[shard][places], right_factor[shard][places], left_basis[shard][places], right_basis[shard][places], first_moment[shard][places], second_moment[shard][places])
        lefts.append(left_factor[shard].at[places].set(results[0]))
        rights.append(right_factor[shard].at[places].set(results[1]))
        firsts.append(first_moment[shard].at[places].set(results[2]))
        seconds.append(second_moment[shard].at[places].set(results[3]))
        updates.append(results[4])
    return (jnp.stack(updates), jnp.stack(lefts), jnp.stack(rights), jnp.stack(firsts), jnp.stack(seconds))
```

```python
import functools

import jax
import jax.numpy as jnp
from jax import lax
from jax.experimental import pallas as pl
from jax.experimental.pallas import tpu as pltpu
from jax.sharding import Mesh
from jax.sharding import PartitionSpec as P

BLOCK = 256
TILE_ROWS = 16
TILE_COLS = 128
Y, X, CORE = 4, 4, 2
N_DP = Y * X * CORE
N_TENSOR = 8
ROW = X * CORE
SLOTS = 5
HOME = 4
NBLK = 128
ROW_BLOCKS = 16
COL_BLOCKS = 8
LOCAL_ROWS = ROW_BLOCKS // ROW
LOCAL_BLOCKS = LOCAL_ROWS * COL_BLOCKS
TOK_SUB = 32
DP = ("y", "x", "core")
ROW_AXES = ("x", "core")

factor_decay = 0.9
first_decay = 0.95
second_decay = 0.95
epsilon_value = 1e-08

PARAMS = pltpu.CompilerParams(vmem_limit_bytes=40 * 1024 * 1024)


def tile_of(m):
    return (
        slice(TILE_ROWS * (m // 2), TILE_ROWS * (m // 2 + 1)),
        slice(TILE_COLS * (m % 2), TILE_COLS * (m % 2 + 1)),
    )


def gradient_kernel(order, *refs):
    whole, halves, grads, out = refs[:7], refs[7:9], refs[9], refs[10]
    total = None
    for j in range(N_TENSOR):
        if j < 7:
            left = whole[j][...]
        else:
            left = jnp.concatenate([halves[0][...], halves[1][...]], axis=1)
        right = grads[:, order[j]].reshape(ROW * TOK_SUB, BLOCK)
        term = jnp.dot(left, right, preferred_element_type=jnp.float32)
        total = term if total is None else total + term
    result = total.astype(jnp.bfloat16)
    for rr in range(LOCAL_ROWS):
        block = result[rr * BLOCK : (rr + 1) * BLOCK]
        for m in range(N_DP):
            rows, cols = tile_of(m)
            out[m, rr] = block[rows, cols]


def gradient_tiles(order, whole, halves, grads):
    resident = lambda a: pl.BlockSpec(a.shape, lambda c, order: (0, 0))
    return pl.pallas_call(
        gradient_kernel,
        grid_spec=pltpu.PrefetchScalarGridSpec(
            num_scalar_prefetch=1,
            grid=(COL_BLOCKS,),
            in_specs=[resident(a) for a in (*whole, *halves)]
            + [
                pl.BlockSpec(
                    (ROW, N_TENSOR, TOK_SUB, BLOCK), lambda c, order: (0, 0, 0, c)
                )
            ],
            out_specs=pl.BlockSpec(
                (N_DP, LOCAL_ROWS, TILE_ROWS, TILE_COLS), lambda c, order: (0, c, 0, 0)
            ),
        ),
        out_shape=jax.ShapeDtypeStruct(
            (N_DP, LOCAL_BLOCKS, TILE_ROWS, TILE_COLS), jnp.bfloat16
        ),
        compiler_params=PARAMS,
        name="gradient_tiles",
    )(order, *whole, *halves, grads)


def to_slots_kernel(slot, parts, out):
    out[...] = jnp.zeros_like(out)

    def body(k, carry):
        c, r = k // ROW_BLOCKS, k % ROW_BLOCKS
        source, place = r // LOCAL_ROWS, c * LOCAL_ROWS + r % LOCAL_ROWS
        total = parts[source, place].astype(jnp.float32)
        for y in range(1, Y):
            total = total + parts[y * ROW + source, place].astype(jnp.float32)
        out[slot[k]] = total.astype(jnp.bfloat16)
        return carry

    lax.fori_loop(0, NBLK, body, 0, unroll=4)


def to_slots(slot, parts):
    return pl.pallas_call(
        to_slots_kernel,
        grid_spec=pltpu.PrefetchScalarGridSpec(
            num_scalar_prefetch=1,
            grid=(1,),
            in_specs=[pl.BlockSpec(parts.shape, lambda i, slot: (0, 0, 0, 0))],
            out_specs=pl.BlockSpec(
                (N_DP * SLOTS, TILE_ROWS, TILE_COLS), lambda i, slot: (0, 0, 0)
            ),
        ),
        out_shape=jax.ShapeDtypeStruct((N_DP * SLOTS, TILE_ROWS, TILE_COLS), jnp.bfloat16),
        compiler_params=PARAMS,
        name="to_slots",
    )(slot, parts)


def from_slots_kernel(slot, tiles, out):
    def body(k, carry):
        out[k] = tiles[slot[k]]
        return carry

    lax.fori_loop(0, NBLK, body, 0, unroll=8)


def from_slots(slot, tiles):
    return pl.pallas_call(
        from_slots_kernel,
        grid_spec=pltpu.PrefetchScalarGridSpec(
            num_scalar_prefetch=1,
            grid=(1,),
            in_specs=[pl.BlockSpec(tiles.shape, lambda i, slot: (0, 0, 0))],
            out_specs=pl.BlockSpec((NBLK, TILE_ROWS, TILE_COLS), lambda i, slot: (0, 0, 0)),
        ),
        out_shape=jax.ShapeDtypeStruct((NBLK, TILE_ROWS, TILE_COLS), jnp.bfloat16),
        compiler_params=PARAMS,
        name="from_slots",
    )(slot, tiles)


def assemble_kernel(tiles, out):
    for h in range(HOME):
        for m in range(N_DP):
            rows, cols = tile_of(m)
            out[0, h, rows, cols] = tiles[m, h]


def assemble(tiles):
    return pl.pallas_call(
        assemble_kernel,
        out_shape=jax.ShapeDtypeStruct((1, HOME, BLOCK, BLOCK), jnp.bfloat16),
        compiler_params=PARAMS,
        name="assemble",
    )(tiles)


def dot(a, b, ca, cb):
    return lax.dot_general(a, b, (((ca,), (cb,)), ((), ())), preferred_element_type=jnp.float32)


def soap_kernel(
    live, tiles, left, right, basis_left, basis_right, first, second,
    update, left_new, right_new, first_new, second_new, gradient,
):
    alive = live[pl.program_id(0)] > 0
    for m in range(N_DP):
        rows, cols = tile_of(m)
        gradient[rows, cols] = tiles[m, 0]
    grad = gradient[...]
    ql, qr = basis_left[0, 0], basis_right[0, 0]
    halfway = dot(ql, grad, 0, 0).astype(jnp.bfloat16)
    rotated = dot(halfway, qr, 1, 0)
    first_old, second_old = first[0, 0], second[0, 0]
    first_float = first_decay * first_old.astype(jnp.float32) + (1.0 - first_decay) * rotated
    second_float = (
        second_decay * second_old.astype(jnp.float32)
        + (1.0 - second_decay) * rotated * rotated
    )
    ratio = (first_float / (jnp.sqrt(second_float) + epsilon_value)).astype(jnp.bfloat16)
    turned = dot(ql, ratio, 1, 0).astype(jnp.bfloat16)
    result = dot(turned, qr, 1, 1).astype(jnp.bfloat16)
    for m in range(N_DP):
        rows, cols = tile_of(m)
        update[m, 0] = result[rows, cols]
    first_new[0, 0] = jnp.where(alive, first_float.astype(jnp.bfloat16), first_old)
    second_new[0, 0] = jnp.where(alive, second_float.astype(jnp.bfloat16), second_old)
    scale = (1.0 - factor_decay) / BLOCK
    left_old, right_old = left[0, 0], right[0, 0]
    left_new[0, 0] = jnp.where(
        alive, factor_decay * left_old + scale * dot(grad, grad, 1, 1), left_old
    )
    right_new[0, 0] = jnp.where(
        alive, factor_decay * right_old + scale * dot(grad, grad, 0, 0), right_old
    )


def soap(live, tiles, left, right, basis_left, basis_right, first, second):
    state = pl.BlockSpec((1, 1, BLOCK, BLOCK), lambda s, live: (0, s, 0, 0))
    pieces = pl.BlockSpec((N_DP, 1, TILE_ROWS, TILE_COLS), lambda s, live: (0, s, 0, 0))
    like = lambda a: jax.ShapeDtypeStruct(a.shape, a.dtype)
    return pl.pallas_call(
        soap_kernel,
        grid_spec=pltpu.PrefetchScalarGridSpec(
            num_scalar_prefetch=1,
            grid=(SLOTS,),
            in_specs=[pieces] + [state] * 6,
            out_specs=[pieces] + [state] * 4,
            scratch_shapes=[pltpu.VMEM((BLOCK, BLOCK), jnp.bfloat16)],
        ),
        out_shape=[like(tiles), like(left), like(right), like(first), like(second)],
        compiler_params=PARAMS,
        name="soap",
    )(live, tiles, left, right, basis_left, basis_right, first, second)


def spread(array, axes):
    return lax.all_to_all(array, axes, split_axis=0, concat_axis=0, tiled=True)


def ring_tokens(mine):
    up = [(i, (i + 1) % N_TENSOR) for i in range(N_TENSOR)]
    down = [(i, (i - 1) % N_TENSOR) for i in range(N_TENSOR)]
    from_below, from_above = mine, mine
    whole = [mine]
    for _ in range(N_TENSOR // 2 - 1):
        from_below = lax.ppermute(from_below, "z", up)
        from_above = lax.ppermute(from_above, "z", down)
        whole += [from_below, from_above]
    half = mine.shape[1] // 2
    halves = [
        lax.ppermute(from_below[:, :half], "z", up),
        lax.ppermute(from_above[:, half:], "z", down),
    ]
    place = lax.axis_index("z")
    steps = jnp.array([0, -1, 1, -2, 2, -3, 3, 4], jnp.int32)
    order = (place + steps + N_TENSOR) % N_TENSOR
    return order, whole, halves


def local(
    tokens, grad_out, owner, left_factor, right_factor,
    left_basis, right_basis, first_moment, second_moment,
):
    owner_row = owner[0]
    block_ids = jnp.arange(NBLK, dtype=jnp.int32)
    same = owner_row[:, None] == owner_row[None, :]
    before = block_ids[None, :] < block_ids[:, None]
    rank = jnp.sum((same & before).astype(jnp.int32), axis=1)
    slot = owner_row * SLOTS + rank
    held = jnp.sum((owner_row == lax.axis_index(DP)).astype(jnp.int32))
    live = (jnp.arange(SLOTS, dtype=jnp.int32) < held).astype(jnp.int32)

    grads = lax.all_gather(grad_out, ROW_AXES, axis=0, tiled=True)
    grads = grads.reshape(ROW, N_TENSOR, TOK_SUB, grad_out.shape[1])
    width = tokens.shape[1] // ROW
    cut = tokens.reshape(TOK_SUB, ROW, width).transpose(1, 0, 2)
    mine = spread(cut, ROW_AXES).transpose(2, 0, 1).reshape(width, ROW * TOK_SUB)
    order, whole, halves = ring_tokens(mine)
    partial = gradient_tiles(order, whole, halves, grads)
    tiles = to_slots(slot, spread(partial, DP))
    tiles = tiles.reshape(N_DP, SLOTS, TILE_ROWS, TILE_COLS)
    update, left_new, right_new, first_new, second_new = soap(
        live, spread(tiles, DP), left_factor, right_factor,
        left_basis, right_basis, first_moment, second_moment,
    )
    back = spread(update, DP).reshape(N_DP * SLOTS, TILE_ROWS, TILE_COLS)
    picked = from_slots(slot, back).reshape(N_DP, HOME, TILE_ROWS, TILE_COLS)
    home_update = assemble(spread(picked, DP))
    return (home_update, left_new, right_new, first_new, second_new)


def solution(mesh):
    split = Mesh(mesh.devices.reshape(Y, X, CORE, N_TENSOR), ("y", "x", "core", "z"))
    state = P("z", DP, None, None)
    return jax.shard_map(
        local,
        mesh=split,
        in_specs=(P((*DP, "z"), None), P(DP, "z"), P("z", None)) + (state,) * 6,
        out_specs=(state,) * 5,
        check_vma=False,
    )
```

```python
import jax
import jax.numpy as jnp
from jax import lax
from jax.experimental import pallas as pl
from jax.experimental.pallas import tpu as pltpu
from jax.sharding import Mesh
from jax.sharding import PartitionSpec as P

BLOCK = 256
TILE_ROWS = 16
TILE_COLS = 128
Y, X, CORE = 4, 4, 2
N_DP = Y * X * CORE
N_TENSOR = 8
ROW = X * CORE
STRIP = BLOCK // ROW
SLOTS = 5
HOME = 4
NBLK = 128
ROW_BLOCKS = 16
COL_BLOCKS = 8
TOK_SUB = 32
LOCAL_ROWS = ROW_BLOCKS * STRIP
DP = ("y", "x", "core")
CHIP_ROWS = LOCAL_ROWS * CORE
SHARD_K = X * TOK_SUB
WIDE = 2
CHUNK_K = NBLK // 2

factor_decay = 0.9
first_decay = 0.95
second_decay = 0.95
epsilon_value = 1e-08

MIB = 1024 * 1024
SMEM = pl.BlockSpec(memory_space=pltpu.SMEM)
VMEM = pl.BlockSpec(memory_space=pltpu.VMEM)


def params(mib):
    return pltpu.CompilerParams(vmem_limit_bytes=mib * MIB)


def tile_of(m):
    y, strip = m // ROW, m % ROW
    top, side = STRIP * strip + TILE_ROWS * (y // 2), TILE_COLS * (y % 2)
    return slice(top, top + TILE_ROWS), slice(side, side + TILE_COLS)


def cut_kernel(core, tokens, out):
    def strips_from(first):
        for chip in range(X):
            for i in range(CORE):
                start = STRIP * (chip * CORE + (first + i) % CORE)
                out[chip, :, i * LOCAL_ROWS : (i + 1) * LOCAL_ROWS] = jnp.concatenate(
                    [
                        tokens[:, r * BLOCK + start : r * BLOCK + start + STRIP]
                        for r in range(ROW_BLOCKS)
                    ],
                    axis=1,
                )

    for first in range(CORE):
        pl.when(core[0] == first)(lambda: strips_from(first))


def cut_tokens(core, tokens):
    return pl.pallas_call(
        cut_kernel,
        in_specs=[SMEM, VMEM],
        out_shape=jax.ShapeDtypeStruct((X, TOK_SUB, CHIP_ROWS), jnp.bfloat16),
        compiler_params=params(32),
        name="cut_tokens",
    )(core, tokens)


def turn_kernel(source, pieces, out):
    joined = jnp.concatenate([pieces[source[i]] for i in range(X)], axis=0)
    out[...] = joined.T


def turn(source, pieces):
    return pl.pallas_call(
        turn_kernel,
        in_specs=[SMEM, VMEM],
        out_shape=jax.ShapeDtypeStruct((CHIP_ROWS, SHARD_K), jnp.bfloat16),
        compiler_params=params(32),
        name="turn",
    )(source, pieces)


def gradient_kernel(place, *refs):
    whole, halves, sources = refs[:7], refs[7:9], refs[9:13]
    outs, (left, right) = refs[13:15], refs[15:]

    @pl.when(pl.program_id(0) == 0)
    def join_tokens():
        for j in range(7):
            left[:, j * SHARD_K : (j + 1) * SHARD_K] = whole[j][...]
        left[:LOCAL_ROWS, 7 * SHARD_K :] = halves[0][...]
        left[LOCAL_ROWS:, 7 * SHARD_K :] = halves[1][...]

    for j in range(N_TENSOR):
        for i in range(X):
            top = j * SHARD_K + i * TOK_SUB
            right[top : top + TOK_SUB] = sources[i][place[j]]
    for column in range(WIDE):
        blocks = slice(column * ROW_BLOCKS, (column + 1) * ROW_BLOCKS)
        result = jnp.dot(
            left[...], right[:, column * BLOCK : (column + 1) * BLOCK],
            preferred_element_type=jnp.float32,
        ).astype(jnp.bfloat16)
        for out, part in zip(outs, (result[:LOCAL_ROWS], result[LOCAL_ROWS:])):
            out[blocks] = part.reshape(ROW_BLOCKS, STRIP, BLOCK)


def gradient_strips(chunk, place, lefts, near, far):
    resident = lambda a: pl.BlockSpec(a.shape, lambda c, place: (0, 0))
    steps = COL_BLOCKS // 2 // WIDE
    shape = (N_TENSOR, TOK_SUB, WIDE * BLOCK)
    near_spec = pl.BlockSpec(shape, lambda c, place: (0, 0, steps * chunk + c))
    far_spec = pl.BlockSpec(shape, lambda c, place: (0, 0, c))
    strips = pl.BlockSpec((WIDE * ROW_BLOCKS, STRIP, BLOCK), lambda c, place: (c, 0, 0))
    return pl.pallas_call(
        gradient_kernel,
        grid_spec=pltpu.PrefetchScalarGridSpec(
            num_scalar_prefetch=1,
            grid=(steps,),
            in_specs=[resident(a) for a in lefts] + [near_spec] * 3 + [far_spec],
            out_specs=[strips] * CORE,
            scratch_shapes=[
                pltpu.VMEM((CHIP_ROWS, N_TENSOR * SHARD_K), jnp.bfloat16),
                pltpu.VMEM((N_TENSOR * SHARD_K, WIDE * BLOCK), jnp.bfloat16),
            ],
        ),
        out_shape=[jax.ShapeDtypeStruct((CHUNK_K, STRIP, BLOCK), jnp.bfloat16)] * CORE,
        compiler_params=params(60),
        cost_estimate=pl.CostEstimate(
            flops=2 * CHIP_ROWS * N_TENSOR * SHARD_K * 4 * BLOCK,
            bytes_accessed=8 * MIB, transcendentals=0,
        ),
        name="gradient_strips",
    )(place, *lefts, *near, far)


def to_slots_kernel(slot, *refs):
    out = refs[-1]
    out[...] = jnp.zeros_like(out)
    for chunk in range(2):
        one, two = refs[2 * chunk : 2 * chunk + 2]

        def body(k, carry):
            total = one[k].astype(jnp.float32) + two[k].astype(jnp.float32)
            out[slot[chunk * CHUNK_K + k]] = total.astype(jnp.bfloat16)
            return carry

        lax.fori_loop(0, CHUNK_K, body, 0, unroll=8)


def to_slots(slot, parts):
    return pl.pallas_call(
        to_slots_kernel,
        in_specs=[SMEM] + [VMEM] * len(parts),
        out_shape=jax.ShapeDtypeStruct((N_DP * SLOTS, STRIP, BLOCK), jnp.bfloat16),
        compiler_params=params(32),
        name="to_slots",
    )(slot, *parts)


def from_slots_kernel(slot, tiles, out):
    def body(k, carry):
        out[k] = tiles[slot[k]]
        return carry

    lax.fori_loop(0, NBLK, body, 0, unroll=8)


def from_slots(slot, tiles):
    return pl.pallas_call(
        from_slots_kernel,
        in_specs=[SMEM, VMEM],
        out_shape=jax.ShapeDtypeStruct((NBLK, TILE_ROWS, TILE_COLS), jnp.bfloat16),
        compiler_params=params(32),
        name="from_slots",
    )(slot, tiles)


def assemble_kernel(tiles, out):
    for h in range(HOME):
        for m in range(N_DP):
            rows, cols = tile_of(m)
            out[0, h, rows, cols] = tiles[m, h]


def assemble(tiles):
    return pl.pallas_call(
        assemble_kernel,
        out_shape=jax.ShapeDtypeStruct((1, HOME, BLOCK, BLOCK), jnp.bfloat16),
        compiler_params=params(32),
        name="assemble",
    )(tiles)


def dot(a, b, ca, cb):
    return lax.dot_general(a, b, (((ca,), (cb,)), ((), ())), preferred_element_type=jnp.float32)


def update_kernel(
    live, strips, basis_left, basis_right, first, second,
    update, grads, first_new, second_new,
):
    for s in range(SLOTS):
        for strip in range(ROW):
            total = strips[strip, s].astype(jnp.float32)
            for y in range(1, Y):
                total = total + strips[y * ROW + strip, s].astype(jnp.float32)
            grads[s, strip * STRIP : (strip + 1) * STRIP] = total.astype(jnp.bfloat16)
        grad = grads[s]
        ql, qr = basis_left[0, s], basis_right[0, s]
        halfway = dot(ql, grad, 0, 0).astype(jnp.bfloat16)
        rotated = dot(halfway, qr, 1, 0)
        first_old, second_old = first[0, s], second[0, s]
        first_float = first_decay * first_old.astype(jnp.float32) + (1.0 - first_decay) * rotated
        second_float = (
            second_decay * second_old.astype(jnp.float32)
            + (1.0 - second_decay) * rotated * rotated
        )
        ratio = (first_float / (jnp.sqrt(second_float) + epsilon_value)).astype(jnp.bfloat16)
        turned = dot(ql, ratio, 1, 0).astype(jnp.bfloat16)
        result = dot(turned, qr, 1, 1).astype(jnp.bfloat16)
        for m in range(N_DP):
            rows, cols = tile_of(m)
            update[m, s] = result[rows, cols]
        alive = live[s] > 0
        first_new[0, s] = jnp.where(alive, first_float.astype(jnp.bfloat16), first_old)
        second_new[0, s] = jnp.where(alive, second_float.astype(jnp.bfloat16), second_old)


def update_blocks(live, strips, basis_left, basis_right, first, second):
    like = lambda a: jax.ShapeDtypeStruct(a.shape, a.dtype)
    return pl.pallas_call(
        update_kernel,
        in_specs=[SMEM] + [VMEM] * 5,
        out_shape=[
            jax.ShapeDtypeStruct((N_DP, SLOTS, TILE_ROWS, TILE_COLS), jnp.bfloat16),
            jax.ShapeDtypeStruct((SLOTS, BLOCK, BLOCK), jnp.bfloat16),
            like(first),
            like(second),
        ],
        compiler_params=params(60),
        name="update",
    )(live, strips, basis_left, basis_right, first, second)


def factor_kernel(live, grads, left, right, left_new, right_new):
    alive = live[pl.program_id(0)] > 0
    grad = grads[0]
    scale = (1.0 - factor_decay) / BLOCK
    left_old, right_old = left[0, 0], right[0, 0]
    left_new[0, 0] = jnp.where(
        alive, factor_decay * left_old + scale * dot(grad, grad, 1, 1), left_old
    )
    right_new[0, 0] = jnp.where(
        alive, factor_decay * right_old + scale * dot(grad, grad, 0, 0), right_old
    )


def update_factors(live, grads, left, right):
    state = pl.BlockSpec((1, 1, BLOCK, BLOCK), lambda s, live: (0, s, 0, 0))
    return pl.pallas_call(
        factor_kernel,
        grid_spec=pltpu.PrefetchScalarGridSpec(
            num_scalar_prefetch=1,
            grid=(SLOTS,),
            in_specs=[pl.BlockSpec((1, BLOCK, BLOCK), lambda s, live: (s, 0, 0))] + [state] * 2,
            out_specs=[state] * 2,
        ),
        out_shape=[jax.ShapeDtypeStruct(a.shape, a.dtype) for a in (left, right)],
        compiler_params=params(60),
        cost_estimate=pl.CostEstimate(
            flops=4 * SLOTS * BLOCK**3, bytes_accessed=6 * MIB, transcendentals=0
        ),
        name="factors",
    )(live, grads, left, right)


def spread(array, axes):
    return lax.all_to_all(array, axes, split_axis=0, concat_axis=0, tiled=True)


def ring(size, step):
    return [(i, (i + step) % size) for i in range(size)]


def gather_row(tokens, grads, source, core):
    up, down = ring(N_TENSOR, 1), ring(N_TENSOR, -1)
    ahead, back = ring(X, 1), ring(X, -1)

    pieces, grads = lax.optimization_barrier((spread(cut_tokens(core, tokens), "x"), grads))
    behind, before = lax.ppermute(grads, "x", ahead), lax.ppermute(grads, "x", back)
    mine = turn(source, pieces)
    below, above = lax.ppermute(mine, "z", up), lax.ppermute(mine, "z", down)
    whole = [mine, below, above]
    below, above = lax.ppermute(below, "z", up), lax.ppermute(above, "z", down)
    whole += [below, above]
    behind, before, below, above = lax.optimization_barrier((behind, before, below, above))
    half = grads.shape[-1] // 2
    far = [
        lax.ppermute(behind[..., :half], "x", ahead),
        lax.ppermute(before[..., half:], "x", back),
    ]
    below, above = lax.ppermute(below, "z", up), lax.ppermute(above, "z", down)
    whole += [below, above]
    halves = [
        lax.ppermute(below[:LOCAL_ROWS], "z", up),
        lax.ppermute(above[LOCAL_ROWS:], "z", down),
    ]
    return whole + halves, [grads, behind, before], far


def local(
    tokens, grad_out, owner, left_factor, right_factor,
    left_basis, right_basis, first_moment, second_moment,
):
    owner_row = owner[0]
    block_ids = jnp.arange(NBLK, dtype=jnp.int32)
    same = owner_row[:, None] == owner_row[None, :]
    before = block_ids[None, :] < block_ids[:, None]
    rank = jnp.sum((same & before).astype(jnp.int32), axis=1)
    slot = owner_row * SLOTS + rank
    held = jnp.sum((owner_row == lax.axis_index(DP)).astype(jnp.int32))
    live = (jnp.arange(SLOTS, dtype=jnp.int32) < held).astype(jnp.int32)

    steps = jnp.array([0, -1, 1, -2, 2, -3, 3, 4], jnp.int32)
    place = (lax.axis_index("z") + steps + N_TENSOR) % N_TENSOR
    along = jnp.array([0, -1, 1, 2], jnp.int32)
    source = (lax.axis_index("x") + along + X) % X
    core = lax.axis_index("core").astype(jnp.int32).reshape(1)
    grads = grad_out.reshape(N_TENSOR, TOK_SUB, grad_out.shape[1])
    lefts, near, far = gather_row(tokens, grads, source, core)
    parts = []
    for chunk in range(2):
        mine, other = gradient_strips(chunk, place, lefts, near, far[chunk])
        parts += [mine, lax.ppermute(other, "core", ring(CORE, 1))]
    strips = to_slots(slot, parts).reshape(N_DP, SLOTS, STRIP, BLOCK)
    update, grad_blocks, first_new, second_new = update_blocks(
        live, spread(strips, DP), left_basis, right_basis, first_moment, second_moment
    )
    left_new, right_new = update_factors(live, grad_blocks, left_factor, right_factor)
    back = spread(update, DP).reshape(N_DP * SLOTS, TILE_ROWS, TILE_COLS)
    picked = from_slots(slot, back).reshape(N_DP, HOME, TILE_ROWS, TILE_COLS)
    home_update = assemble(spread(picked, DP))
    return (home_update, left_new, right_new, first_new, second_new)


def solution(mesh):
    split = Mesh(mesh.devices.reshape(Y, X, CORE, N_TENSOR), ("y", "x", "core", "z"))
    state = P("z", DP, None, None)
    return jax.shard_map(
        local,
        mesh=split,
        in_specs=(P((*DP, "z"), None), P(DP, "z"), P("z", None)) + (state,) * 6,
        out_specs=(state,) * 5,
        check_vma=False,
    )
```

```python
import jax
import jax.numpy as jnp
from jax import lax
from jax.experimental import pallas as pl
from jax.experimental.pallas import tpu as pltpu
from jax.sharding import Mesh
from jax.sharding import PartitionSpec as P

BLOCK = 256
TILE_ROWS = 16
TILE_COLS = 128
Y, X, CORE = 4, 4, 2
N_DP = Y * X * CORE
N_TENSOR = 8
ROW = X * CORE
STRIP = BLOCK // ROW
SLOTS = 5
HOME = 4
NBLK = 128
ROW_BLOCKS = 16
COL_BLOCKS = 8
TOK_SUB = 32
LOCAL_ROWS = ROW_BLOCKS * STRIP
DP = ("y", "x", "core")
SHARD_K = ROW * TOK_SUB
SOURCES = ((0, 0), (0, 1), (-1, 0), (-1, 1), (1, 0), (1, 1), (2, 0), (2, 1))
WIDE = 2
CHUNK_K = NBLK // 2

factor_decay = 0.9
first_decay = 0.95
second_decay = 0.95
epsilon_value = 1e-08

MIB = 1024 * 1024
SMEM = pl.BlockSpec(memory_space=pltpu.SMEM)
VMEM = pl.BlockSpec(memory_space=pltpu.VMEM)


def params(mib):
    return pltpu.CompilerParams(vmem_limit_bytes=mib * MIB)


def tile_of(m):
    y, strip = m // ROW, m % ROW
    top, side = STRIP * strip + TILE_ROWS * (y // 2), TILE_COLS * (y % 2)
    return slice(top, top + TILE_ROWS), slice(side, side + TILE_COLS)


def cut_kernel(tokens, out):
    for strip in range(ROW):
        out[strip] = jnp.concatenate(
            [
                tokens[:, r * BLOCK + STRIP * strip : r * BLOCK + STRIP * (strip + 1)]
                for r in range(ROW_BLOCKS)
            ],
            axis=1,
        )


def cut_tokens(tokens):
    return pl.pallas_call(
        cut_kernel,
        out_shape=jax.ShapeDtypeStruct((ROW, TOK_SUB, LOCAL_ROWS), jnp.bfloat16),
        compiler_params=params(32),
        name="cut_tokens",
    )(tokens)


def turn_kernel(spot, pieces, out):
    places = [
        (spot[1] + dx + X) % X * CORE + (spot[2] + dc) % CORE for dx, dc in SOURCES
    ]
    out[...] = jnp.concatenate([pieces[place] for place in places], axis=0).T


def turn(spot, pieces):
    return pl.pallas_call(
        turn_kernel,
        in_specs=[SMEM, VMEM],
        out_shape=jax.ShapeDtypeStruct((LOCAL_ROWS, SHARD_K), jnp.bfloat16),
        compiler_params=params(32),
        name="turn",
    )(spot, pieces)


def gradient_kernel(spot, *refs):
    whole, halves, sources = refs[:7], refs[7:9], refs[9:17]
    outs, (left, right, tiles) = refs[17:21], refs[21:]

    @pl.when(pl.program_id(0) == 0)
    def join_tokens():
        for j in range(7):
            left[:, j * SHARD_K : (j + 1) * SHARD_K] = whole[j][...]
        middle = 7 * SHARD_K + SHARD_K // 2
        left[:, 7 * SHARD_K : middle] = halves[0][...]
        left[:, middle:] = halves[1][...]

    for j, step in enumerate((0, -1, 1, -2, 2, -3, 3, 4)):
        place = (spot[3] + step + N_TENSOR) % N_TENSOR
        for i in range(ROW):
            top = j * SHARD_K + i * TOK_SUB
            right[top : top + TOK_SUB] = sources[i][place]
    for column in range(WIDE):
        result = jnp.dot(
            left[...], right[:, column * BLOCK : (column + 1) * BLOCK],
            preferred_element_type=jnp.float32,
        ).astype(jnp.bfloat16)
        for r in range(ROW_BLOCKS):
            for y in range(Y):
                rows, cols = tile_of(y * ROW)
                top = r * STRIP + rows.start
                tiles[y, column * ROW_BLOCKS + r] = result[top : top + TILE_ROWS, cols]
    for step in range(Y):
        outs[step][...] = tiles[(spot[0] + step) % Y]


def gradient_tiles(chunk, spot, lefts, near, far):
    resident = lambda a: pl.BlockSpec(a.shape, lambda c, spot: (0, 0))
    steps = COL_BLOCKS // 2 // WIDE
    blocks = WIDE * ROW_BLOCKS
    shape = (N_TENSOR, TOK_SUB, WIDE * BLOCK)
    near_spec = pl.BlockSpec(shape, lambda c, spot: (0, 0, steps * chunk + c))
    far_spec = pl.BlockSpec(shape, lambda c, spot: (0, 0, c))
    part = pl.BlockSpec((blocks, TILE_ROWS, TILE_COLS), lambda c, spot: (c, 0, 0))
    return pl.pallas_call(
        gradient_kernel,
        grid_spec=pltpu.PrefetchScalarGridSpec(
            num_scalar_prefetch=1,
            grid=(steps,),
            in_specs=[resident(a) for a in lefts] + [near_spec] * 6 + [far_spec] * 2,
            out_specs=[part] * Y,
            scratch_shapes=[
                pltpu.VMEM((LOCAL_ROWS, N_TENSOR * SHARD_K), jnp.bfloat16),
                pltpu.VMEM((N_TENSOR * SHARD_K, WIDE * BLOCK), jnp.bfloat16),
                pltpu.VMEM((Y, blocks, TILE_ROWS, TILE_COLS), jnp.bfloat16),
            ],
        ),
        out_shape=[jax.ShapeDtypeStruct((CHUNK_K, TILE_ROWS, TILE_COLS), jnp.bfloat16)] * Y,
        compiler_params=params(60),
        cost_estimate=pl.CostEstimate(
            flops=2 * LOCAL_ROWS * N_TENSOR * SHARD_K * 4 * BLOCK,
            bytes_accessed=8 * MIB, transcendentals=0,
        ),
        name="gradient_tiles",
    )(spot, *lefts, *near, *far)


def to_slots_kernel(slot, *refs):
    out = refs[-1]
    out[...] = jnp.zeros_like(out)
    for chunk in range(2):
        mine, *others = refs[Y * chunk : Y * (chunk + 1)]

        def body(k, carry):
            total = mine[k].astype(jnp.float32)
            for part in others:
                total = total + part[k].astype(jnp.float32)
            out[slot[chunk * CHUNK_K + k]] = total.astype(jnp.bfloat16)
            return carry

        lax.fori_loop(0, CHUNK_K, body, 0, unroll=8)


def to_slots(slot, parts):
    return pl.pallas_call(
        to_slots_kernel,
        in_specs=[SMEM] + [VMEM] * len(parts),
        out_shape=jax.ShapeDtypeStruct((N_DP * SLOTS, TILE_ROWS, TILE_COLS), jnp.bfloat16),
        compiler_params=params(32),
        name="to_slots",
    )(slot, *parts)


def from_slots_kernel(slot, tiles, out):
    def body(k, carry):
        out[k] = tiles[slot[k]]
        return carry

    lax.fori_loop(0, NBLK, body, 0, unroll=8)


def from_slots(slot, tiles):
    return pl.pallas_call(
        from_slots_kernel,
        grid_spec=pltpu.PrefetchScalarGridSpec(
            num_scalar_prefetch=1,
            grid=(1,),
            in_specs=[pl.BlockSpec(tiles.shape, lambda i, slot: (0, 0, 0))],
            out_specs=pl.BlockSpec((NBLK, TILE_ROWS, TILE_COLS), lambda i, slot: (0, 0, 0)),
        ),
        out_shape=jax.ShapeDtypeStruct((NBLK, TILE_ROWS, TILE_COLS), jnp.bfloat16),
        compiler_params=params(40),
        name="from_slots",
    )(slot, tiles)


def assemble_kernel(tiles, out):
    for h in range(HOME):
        for m in range(N_DP):
            rows, cols = tile_of(m)
            out[0, h, rows, cols] = tiles[m, h]


def assemble(tiles):
    return pl.pallas_call(
        assemble_kernel,
        out_shape=jax.ShapeDtypeStruct((1, HOME, BLOCK, BLOCK), jnp.bfloat16),
        compiler_params=params(32),
        name="assemble",
    )(tiles)


def dot(a, b, ca, cb):
    return lax.dot_general(a, b, (((ca,), (cb,)), ((), ())), preferred_element_type=jnp.float32)


def update_kernel(
    live, tiles, basis_left, basis_right, first, second,
    update, grads, first_new, second_new,
):
    for s in range(SLOTS):
        for m in range(N_DP):
            rows, cols = tile_of(m)
            grads[s, rows, cols] = tiles[m, s]
        grad = grads[s]
        ql, qr = basis_left[0, s], basis_right[0, s]
        halfway = dot(ql, grad, 0, 0).astype(jnp.bfloat16)
        rotated = dot(halfway, qr, 1, 0)
        first_old, second_old = first[0, s], second[0, s]
        first_float = first_decay * first_old.astype(jnp.float32) + (1.0 - first_decay) * rotated
        second_float = (
            second_decay * second_old.astype(jnp.float32)
            + (1.0 - second_decay) * rotated * rotated
        )
        ratio = (first_float / (jnp.sqrt(second_float) + epsilon_value)).astype(jnp.bfloat16)
        turned = dot(ql, ratio, 1, 0).astype(jnp.bfloat16)
        result = dot(turned, qr, 1, 1).astype(jnp.bfloat16)
        for m in range(N_DP):
            rows, cols = tile_of(m)
            update[m, s] = result[rows, cols]
        alive = live[s] > 0
        first_new[0, s] = jnp.where(alive, first_float.astype(jnp.bfloat16), first_old)
        second_new[0, s] = jnp.where(alive, second_float.astype(jnp.bfloat16), second_old)


def update_blocks(live, tiles, basis_left, basis_right, first, second):
    like = lambda a: jax.ShapeDtypeStruct(a.shape, a.dtype)
    return pl.pallas_call(
        update_kernel,
        in_specs=[SMEM] + [VMEM] * 5,
        out_shape=[
            like(tiles),
            jax.ShapeDtypeStruct((SLOTS, BLOCK, BLOCK), jnp.bfloat16),
            like(first),
            like(second),
        ],
        compiler_params=params(60),
        name="update",
    )(live, tiles, basis_left, basis_right, first, second)


def factor_kernel(live, grads, left, right, left_new, right_new):
    alive = live[pl.program_id(0)] > 0
    grad = grads[0]
    scale = (1.0 - factor_decay) / BLOCK
    left_old, right_old = left[0, 0], right[0, 0]
    left_new[0, 0] = jnp.where(
        alive, factor_decay * left_old + scale * dot(grad, grad, 1, 1), left_old
    )
    right_new[0, 0] = jnp.where(
        alive, factor_decay * right_old + scale * dot(grad, grad, 0, 0), right_old
    )


def update_factors(live, grads, left, right):
    state = pl.BlockSpec((1, 1, BLOCK, BLOCK), lambda s, live: (0, s, 0, 0))
    return pl.pallas_call(
        factor_kernel,
        grid_spec=pltpu.PrefetchScalarGridSpec(
            num_scalar_prefetch=1,
            grid=(SLOTS,),
            in_specs=[pl.BlockSpec((1, BLOCK, BLOCK), lambda s, live: (s, 0, 0))] + [state] * 2,
            out_specs=[state] * 2,
        ),
        out_shape=[jax.ShapeDtypeStruct(a.shape, a.dtype) for a in (left, right)],
        compiler_params=params(60),
        cost_estimate=pl.CostEstimate(
            flops=4 * SLOTS * BLOCK**3, bytes_accessed=6 * MIB, transcendentals=0
        ),
        name="factors",
    )(live, grads, left, right)


def spread(array, axes):
    return lax.all_to_all(array, axes, split_axis=0, concat_axis=0, tiled=True)


def ring(size, step):
    return [(i, (i + step) % size) for i in range(size)]


def gather_row(spot, tokens, grads):
    up, down, swap = ring(N_TENSOR, 1), ring(N_TENSOR, -1), ring(CORE, 1)
    ahead, back = ring(X, 1), ring(X, -1)
    across = lambda a: [a, lax.ppermute(a, "core", swap)]

    pieces, grads = lax.optimization_barrier(
        (spread(cut_tokens(tokens), ("x", "core")), grads)
    )
    behind, before = lax.ppermute(grads, "x", ahead), lax.ppermute(grads, "x", back)
    mine = turn(spot, pieces)
    below, above = lax.ppermute(mine, "z", up), lax.ppermute(mine, "z", down)
    whole = [mine, below, above]
    near = across(grads)
    below, above = lax.ppermute(below, "z", up), lax.ppermute(above, "z", down)
    whole += [below, above]
    behind, before, below, above = lax.optimization_barrier((behind, before, below, above))
    half = grads.shape[-1] // 2
    first = lax.ppermute(behind[..., :half], "x", ahead)
    last = lax.ppermute(before[..., half:], "x", back)
    below, above = lax.ppermute(below, "z", up), lax.ppermute(above, "z", down)
    whole += [below, above]
    near += across(behind) + across(before)
    half = mine.shape[1] // 2
    halves = [
        lax.ppermute(below[:, :half], "z", up),
        lax.ppermute(above[:, half:], "z", down),
    ]
    return whole + halves, near, (across(first), across(last))


def sum_parts(parts):
    return [parts[0]] + [lax.ppermute(parts[step], "y", ring(Y, step)) for step in (2, 1, 3)]


def local(
    tokens, grad_out, owner, left_factor, right_factor,
    left_basis, right_basis, first_moment, second_moment,
):
    owner_row = owner[0]
    block_ids = jnp.arange(NBLK, dtype=jnp.int32)
    same = owner_row[:, None] == owner_row[None, :]
    before = block_ids[None, :] < block_ids[:, None]
    rank = jnp.sum((same & before).astype(jnp.int32), axis=1)
    slot = owner_row * SLOTS + rank
    held = jnp.sum((owner_row == lax.axis_index(DP)).astype(jnp.int32))
    live = (jnp.arange(SLOTS, dtype=jnp.int32) < held).astype(jnp.int32)

    spot = jnp.stack([lax.axis_index(axis) for axis in (*DP, "z")]).astype(jnp.int32)
    grads = grad_out.reshape(N_TENSOR, TOK_SUB, grad_out.shape[1])
    lefts, near, far = gather_row(spot, tokens, grads)
    parts = []
    for chunk in range(2):
        parts += sum_parts(gradient_tiles(chunk, spot, lefts, near, far[chunk]))
    tiles = to_slots(slot, parts).reshape(N_DP, SLOTS, TILE_ROWS, TILE_COLS)
    update, grad_blocks, first_new, second_new = update_blocks(
        live, spread(tiles, DP), left_basis, right_basis, first_moment, second_moment
    )
    left_new, right_new = update_factors(live, grad_blocks, left_factor, right_factor)
    back = spread(update, DP).reshape(N_DP * SLOTS, TILE_ROWS, TILE_COLS)
    picked = from_slots(slot, back).reshape(N_DP, HOME, TILE_ROWS, TILE_COLS)
    home_update = assemble(spread(picked, DP))
    return (home_update, left_new, right_new, first_new, second_new)


def solution(mesh):
    split = Mesh(mesh.devices.reshape(Y, X, CORE, N_TENSOR), ("y", "x", "core", "z"))
    state = P("z", DP, None, None)
    return jax.shard_map(
        local,
        mesh=split,
        in_specs=(P((*DP, "z"), None), P(DP, "z"), P("z", None)) + (state,) * 6,
        out_specs=(state,) * 5,
        check_vma=False,
    )
```

```python
import jax
import jax.numpy as jnp
from jax import lax
from jax.experimental import pallas as pl
from jax.experimental.pallas import tpu as pltpu
from jax.sharding import Mesh
from jax.sharding import PartitionSpec as P

BLOCK = 256
TILE_ROWS = 16
TILE_COLS = 128
Y, X, CORE = 4, 4, 2
N_DP = Y * X * CORE
N_TENSOR = 8
ROW = X * CORE
STRIP = BLOCK // ROW
SLOTS = 5
HOME = 4
NBLK = 128
ROW_BLOCKS = 16
COL_BLOCKS = 8
TOK_SUB = 32
LOCAL_ROWS = ROW_BLOCKS * STRIP
DP = ("y", "x", "core")
CHIP_ROWS = LOCAL_ROWS * CORE
SHARD_K = X * TOK_SUB
SOURCES = (0, -1, 1, 2)
WIDE = 2
CHUNK_K = NBLK // 2

factor_decay = 0.9
first_decay = 0.95
second_decay = 0.95
epsilon_value = 1e-08

MIB = 1024 * 1024
SMEM = pl.BlockSpec(memory_space=pltpu.SMEM)
VMEM = pl.BlockSpec(memory_space=pltpu.VMEM)


def params(mib):
    return pltpu.CompilerParams(vmem_limit_bytes=mib * MIB)


def tile_of(m):
    y, strip = m // ROW, m % ROW
    top, side = STRIP * strip + TILE_ROWS * (y // 2), TILE_COLS * (y % 2)
    return slice(top, top + TILE_ROWS), slice(side, side + TILE_COLS)


def cut_kernel(spot, tokens, out):
    def strips_from(first):
        for chip in range(X):
            for i in range(CORE):
                start = STRIP * (chip * CORE + (first + i) % CORE)
                out[chip, :, i * LOCAL_ROWS : (i + 1) * LOCAL_ROWS] = jnp.concatenate(
                    [
                        tokens[:, r * BLOCK + start : r * BLOCK + start + STRIP]
                        for r in range(ROW_BLOCKS)
                    ],
                    axis=1,
                )

    for first in range(CORE):
        pl.when(spot[2] == first)(lambda: strips_from(first))


def cut_tokens(spot, tokens):
    return pl.pallas_call(
        cut_kernel,
        in_specs=[SMEM, VMEM],
        out_shape=jax.ShapeDtypeStruct((X, TOK_SUB, CHIP_ROWS), jnp.bfloat16),
        compiler_params=params(32),
        name="cut_tokens",
    )(spot, tokens)


def turn_kernel(spot, pieces, out):
    joined = [pieces[(spot[1] + step + X) % X] for step in SOURCES]
    out[...] = jnp.concatenate(joined, axis=0).T


def turn(spot, pieces):
    return pl.pallas_call(
        turn_kernel,
        in_specs=[SMEM, VMEM],
        out_shape=jax.ShapeDtypeStruct((CHIP_ROWS, SHARD_K), jnp.bfloat16),
        compiler_params=params(32),
        name="turn",
    )(spot, pieces)


def gradient_kernel(spot, *refs):
    whole, halves, sources = refs[:7], refs[7:9], refs[9:13]
    mine, other, (left, right, tiles) = refs[13:17], refs[17], refs[18:]

    @pl.when(pl.program_id(0) == 0)
    def join_tokens():
        for j in range(7):
            left[:, j * SHARD_K : (j + 1) * SHARD_K] = whole[j][...]
        left[:LOCAL_ROWS, 7 * SHARD_K :] = halves[0][...]
        left[LOCAL_ROWS:, 7 * SHARD_K :] = halves[1][...]

    for j, step in enumerate((0, -1, 1, -2, 2, -3, 3, 4)):
        place = (spot[3] + step + N_TENSOR) % N_TENSOR
        for i in range(X):
            top = j * SHARD_K + i * TOK_SUB
            right[top : top + TOK_SUB] = sources[i][place]
    for column in range(WIDE):
        result = jnp.dot(
            left[...], right[:, column * BLOCK : (column + 1) * BLOCK],
            preferred_element_type=jnp.float32,
        ).astype(jnp.bfloat16)
        for side in range(CORE):
            for r in range(ROW_BLOCKS):
                for y in range(Y):
                    rows, cols = tile_of(y * ROW)
                    top = side * LOCAL_ROWS + r * STRIP + rows.start
                    tiles[side, y, column * ROW_BLOCKS + r] = result[top : top + TILE_ROWS, cols]
    for step in range(Y):
        place = (spot[0] + step) % Y
        mine[step][...] = tiles[0, place]
        other[step] = tiles[1, place]


def gradient_tiles(chunk, spot, lefts, near, far):
    resident = lambda a: pl.BlockSpec(a.shape, lambda c, spot: (0, 0))
    steps = COL_BLOCKS // 2 // WIDE
    blocks = WIDE * ROW_BLOCKS
    shape = (N_TENSOR, TOK_SUB, WIDE * BLOCK)
    near_spec = pl.BlockSpec(shape, lambda c, spot: (0, 0, steps * chunk + c))
    far_spec = pl.BlockSpec(shape, lambda c, spot: (0, 0, c))
    part = pl.BlockSpec((blocks, TILE_ROWS, TILE_COLS), lambda c, spot: (c, 0, 0))
    return pl.pallas_call(
        gradient_kernel,
        grid_spec=pltpu.PrefetchScalarGridSpec(
            num_scalar_prefetch=1,
            grid=(steps,),
            in_specs=[resident(a) for a in lefts] + [near_spec] * 3 + [far_spec],
            out_specs=[part] * Y
            + [pl.BlockSpec((Y, blocks, TILE_ROWS, TILE_COLS), lambda c, spot: (0, c, 0, 0))],
            scratch_shapes=[
                pltpu.VMEM((CHIP_ROWS, N_TENSOR * SHARD_K), jnp.bfloat16),
                pltpu.VMEM((N_TENSOR * SHARD_K, WIDE * BLOCK), jnp.bfloat16),
                pltpu.VMEM((CORE, Y, blocks, TILE_ROWS, TILE_COLS), jnp.bfloat16),
            ],
        ),
        out_shape=[jax.ShapeDtypeStruct((CHUNK_K, TILE_ROWS, TILE_COLS), jnp.bfloat16)] * Y
        + [jax.ShapeDtypeStruct((Y, CHUNK_K, TILE_ROWS, TILE_COLS), jnp.bfloat16)],
        compiler_params=params(60),
        cost_estimate=pl.CostEstimate(
            flops=2 * CHIP_ROWS * N_TENSOR * SHARD_K * 4 * BLOCK,
            bytes_accessed=8 * MIB, transcendentals=0,
        ),
        name="gradient_tiles",
    )(spot, *lefts, *near, far)


def add_cores_kernel(one, two, three, other, *outs):
    for d, (mine, out) in enumerate(zip((one, two, three), outs), 1):
        out[...] = (mine[...].astype(jnp.float32) + other[d].astype(jnp.float32)).astype(
            jnp.bfloat16
        )


def add_cores(parts, other):
    blocks = CHUNK_K // 4
    part = pl.BlockSpec((blocks, TILE_ROWS, TILE_COLS), lambda c: (c, 0, 0))
    return pl.pallas_call(
        add_cores_kernel,
        grid=(4,),
        in_specs=[part] * 3
        + [pl.BlockSpec((Y, blocks, TILE_ROWS, TILE_COLS), lambda c: (0, c, 0, 0))],
        out_specs=[part] * 3,
        out_shape=[jax.ShapeDtypeStruct(a.shape, a.dtype) for a in parts[1:]],
        compiler_params=params(60),
        name="add_cores",
    )(*parts[1:], other)


def to_slots_kernel(slot, *refs):
    out = refs[-1]
    out[...] = jnp.zeros_like(out)
    for chunk in range(2):
        mine, other, *rest = refs[5 * chunk : 5 * chunk + 5]

        def body(k, carry):
            total = mine[k].astype(jnp.float32) + other[0, k].astype(jnp.float32)
            for part in rest:
                total = total + part[k].astype(jnp.float32)
            out[slot[chunk * CHUNK_K + k]] = total.astype(jnp.bfloat16)
            return carry

        lax.fori_loop(0, CHUNK_K, body, 0, unroll=8)


def to_slots(slot, chunks):
    flat = [a for chunk in chunks for a in chunk]
    return pl.pallas_call(
        to_slots_kernel,
        in_specs=[SMEM] + [VMEM] * len(flat),
        out_shape=jax.ShapeDtypeStruct((N_DP * SLOTS, TILE_ROWS, TILE_COLS), jnp.bfloat16),
        compiler_params=params(32),
        name="to_slots",
    )(slot, *flat)


def from_slots_kernel(slot, tiles, out):
    def body(k, carry):
        out[k] = tiles[slot[k]]
        return carry

    lax.fori_loop(0, NBLK, body, 0, unroll=8)


def from_slots(slot, tiles):
    return pl.pallas_call(
        from_slots_kernel,
        in_specs=[SMEM, VMEM],
        out_shape=jax.ShapeDtypeStruct((NBLK, TILE_ROWS, TILE_COLS), jnp.bfloat16),
        compiler_params=params(32),
        name="from_slots",
    )(slot, tiles)


def assemble_kernel(tiles, out):
    for h in range(HOME):
        for m in range(N_DP):
            rows, cols = tile_of(m)
            out[0, h, rows, cols] = tiles[m, h]


def assemble(tiles):
    return pl.pallas_call(
        assemble_kernel,
        out_shape=jax.ShapeDtypeStruct((1, HOME, BLOCK, BLOCK), jnp.bfloat16),
        compiler_params=params(32),
        name="assemble",
    )(tiles)


def dot(a, b, ca, cb):
    return lax.dot_general(a, b, (((ca,), (cb,)), ((), ())), preferred_element_type=jnp.float32)


def update_kernel(
    live, tiles, basis_left, basis_right, first, second,
    update, grads, first_new, second_new,
):
    for s in range(SLOTS):
        for m in range(N_DP):
            rows, cols = tile_of(m)
            grads[s, rows, cols] = tiles[m, s]
        grad = grads[s]
        ql, qr = basis_left[0, s], basis_right[0, s]
        halfway = dot(ql, grad, 0, 0).astype(jnp.bfloat16)
        rotated = dot(halfway, qr, 1, 0)
        first_old, second_old = first[0, s], second[0, s]
        first_float = first_decay * first_old.astype(jnp.float32) + (1.0 - first_decay) * rotated
        second_float = (
            second_decay * second_old.astype(jnp.float32)
            + (1.0 - second_decay) * rotated * rotated
        )
        ratio = (first_float / (jnp.sqrt(second_float) + epsilon_value)).astype(jnp.bfloat16)
        turned = dot(ql, ratio, 1, 0).astype(jnp.bfloat16)
        result = dot(turned, qr, 1, 1).astype(jnp.bfloat16)
        for m in range(N_DP):
            rows, cols = tile_of(m)
            update[m, s] = result[rows, cols]
        alive = live[s] > 0
        first_new[0, s] = jnp.where(alive, first_float.astype(jnp.bfloat16), first_old)
        second_new[0, s] = jnp.where(alive, second_float.astype(jnp.bfloat16), second_old)


def update_blocks(live, tiles, basis_left, basis_right, first, second):
    like = lambda a: jax.ShapeDtypeStruct(a.shape, a.dtype)
    return pl.pallas_call(
        update_kernel,
        in_specs=[SMEM] + [VMEM] * 5,
        out_shape=[
            like(tiles),
            jax.ShapeDtypeStruct((SLOTS, BLOCK, BLOCK), jnp.bfloat16),
            like(first),
            like(second),
        ],
        compiler_params=params(60),
        name="update",
    )(live, tiles, basis_left, basis_right, first, second)


def factor_kernel(live, grads, left, right, left_new, right_new):
    alive = live[pl.program_id(0)] > 0
    grad = grads[0]
    scale = (1.0 - factor_decay) / BLOCK
    left_old, right_old = left[0, 0], right[0, 0]
    left_new[0, 0] = jnp.where(
        alive, factor_decay * left_old + scale * dot(grad, grad, 1, 1), left_old
    )
    right_new[0, 0] = jnp.where(
        alive, factor_decay * right_old + scale * dot(grad, grad, 0, 0), right_old
    )


def update_factors(live, grads, left, right):
    state = pl.BlockSpec((1, 1, BLOCK, BLOCK), lambda s, live: (0, s, 0, 0))
    return pl.pallas_call(
        factor_kernel,
        grid_spec=pltpu.PrefetchScalarGridSpec(
            num_scalar_prefetch=1,
            grid=(SLOTS,),
            in_specs=[pl.BlockSpec((1, BLOCK, BLOCK), lambda s, live: (s, 0, 0))] + [state] * 2,
            out_specs=[state] * 2,
        ),
        out_shape=[jax.ShapeDtypeStruct(a.shape, a.dtype) for a in (left, right)],
        compiler_params=params(60),
        cost_estimate=pl.CostEstimate(
            flops=4 * SLOTS * BLOCK**3, bytes_accessed=6 * MIB, transcendentals=0
        ),
        name="factors",
    )(live, grads, left, right)


def spread(array, axes):
    return lax.all_to_all(array, axes, split_axis=0, concat_axis=0, tiled=True)


def ring(size, step):
    return [(i, (i + step) % size) for i in range(size)]


def gather_row(spot, tokens, grads):
    up, down = ring(N_TENSOR, 1), ring(N_TENSOR, -1)
    ahead, back = ring(X, 1), ring(X, -1)

    pieces, grads = lax.optimization_barrier((spread(cut_tokens(spot, tokens), "x"), grads))
    behind, before = lax.ppermute(grads, "x", ahead), lax.ppermute(grads, "x", back)
    mine = turn(spot, pieces)
    below, above = lax.ppermute(mine, "z", up), lax.ppermute(mine, "z", down)
    whole = [mine, below, above]
    below, above = lax.ppermute(below, "z", up), lax.ppermute(above, "z", down)
    whole += [below, above]
    behind, before, below, above = lax.optimization_barrier((behind, before, below, above))
    half = grads.shape[-1] // 2
    far = [
        lax.ppermute(behind[..., :half], "x", ahead),
        lax.ppermute(before[..., half:], "x", back),
    ]
    below, above = lax.ppermute(below, "z", up), lax.ppermute(above, "z", down)
    whole += [below, above]
    halves = [
        lax.ppermute(below[:LOCAL_ROWS], "z", up),
        lax.ppermute(above[LOCAL_ROWS:], "z", down),
    ]
    return whole + halves, [grads, behind, before], far


def sum_parts(parts):
    mine, other = parts[:Y], lax.ppermute(parts[Y], "core", ring(CORE, 1))
    one, two, three = add_cores(mine, other)
    moved = [
        lax.ppermute(a, "y", ring(Y, step)) for a, step in ((two, 2), (one, 1), (three, 3))
    ]
    return [mine[0], other] + moved


def local(
    tokens, grad_out, owner, left_factor, right_factor,
    left_basis, right_basis, first_moment, second_moment,
):
    owner_row = owner[0]
    block_ids = jnp.arange(NBLK, dtype=jnp.int32)
    same = owner_row[:, None] == owner_row[None, :]
    before = block_ids[None, :] < block_ids[:, None]
    rank = jnp.sum((same & before).astype(jnp.int32), axis=1)
    slot = owner_row * SLOTS + rank
    held = jnp.sum((owner_row == lax.axis_index(DP)).astype(jnp.int32))
    live = (jnp.arange(SLOTS, dtype=jnp.int32) < held).astype(jnp.int32)

    spot = jnp.stack([lax.axis_index(axis) for axis in (*DP, "z")]).astype(jnp.int32)
    grads = grad_out.reshape(N_TENSOR, TOK_SUB, grad_out.shape[1])
    lefts, near, far = gather_row(spot, tokens, grads)
    chunks = [
        sum_parts(gradient_tiles(chunk, spot, lefts, near, far[chunk])) for chunk in range(2)
    ]
    tiles = to_slots(slot, chunks).reshape(N_DP, SLOTS, TILE_ROWS, TILE_COLS)
    update, grad_blocks, first_new, second_new = update_blocks(
        live, spread(tiles, DP), left_basis, right_basis, first_moment, second_moment
    )
    left_new, right_new = update_factors(live, grad_blocks, left_factor, right_factor)
    back = spread(update, DP).reshape(N_DP * SLOTS, TILE_ROWS, TILE_COLS)
    picked = from_slots(slot, back).reshape(N_DP, HOME, TILE_ROWS, TILE_COLS)
    home_update = assemble(spread(picked, DP))
    return (home_update, left_new, right_new, first_new, second_new)


def solution(mesh):
    split = Mesh(mesh.devices.reshape(Y, X, CORE, N_TENSOR), ("y", "x", "core", "z"))
    state = P("z", DP, None, None)
    return jax.shard_map(
        local,
        mesh=split,
        in_specs=(P((*DP, "z"), None), P(DP, "z"), P("z", None)) + (state,) * 6,
        out_specs=(state,) * 5,
        check_vma=False,
    )
```

```python
import jax
import jax.numpy as jnp
from jax import lax
from jax.experimental import pallas as pl
from jax.experimental.pallas import tpu as pltpu
from jax.sharding import Mesh
from jax.sharding import PartitionSpec as P

BLOCK = 256
TILE_ROWS = 16
TILE_COLS = 128
Y, X, CORE = 4, 4, 2
N_DP = Y * X * CORE
N_TENSOR = 8
ROW = X * CORE
STRIP = BLOCK // ROW
SLOTS = 5
HOME = 4
NBLK = 128
ROW_BLOCKS = 16
COL_BLOCKS = 8
TOK_SUB = 32
LOCAL_ROWS = ROW_BLOCKS * STRIP
DP = ("y", "x", "core")
CHIP_ROWS = LOCAL_ROWS * CORE
SHARD_K = X * TOK_SUB
WIDE = 2
CHUNK_K = NBLK // 2

factor_decay = 0.9
first_decay = 0.95
second_decay = 0.95
epsilon_value = 1e-08

MIB = 1024 * 1024
SMEM = pl.BlockSpec(memory_space=pltpu.SMEM)
VMEM = pl.BlockSpec(memory_space=pltpu.VMEM)


def params(mib):
    return pltpu.CompilerParams(vmem_limit_bytes=mib * MIB)


def tile_of(m):
    y, strip = m // ROW, m % ROW
    top, side = STRIP * strip + TILE_ROWS * (y // 2), TILE_COLS * (y % 2)
    return slice(top, top + TILE_ROWS), slice(side, side + TILE_COLS)


def cut_kernel(spot, tokens, *refs):
    outs, (held, pieces, sem) = refs[:X], refs[X:]
    copy = pltpu.make_async_copy(tokens, held, sem)
    copy.start()
    copy.wait()
    for strip in range(ROW):
        pieces[strip // CORE, strip % CORE] = jnp.concatenate(
            [
                held[:, r * BLOCK + STRIP * strip : r * BLOCK + STRIP * (strip + 1)]
                for r in range(ROW_BLOCKS)
            ],
            axis=1,
        )
    for step in range(X):
        chip = (spot[1] + step) % X
        for i in range(CORE):
            core = (spot[2] + i) % CORE
            outs[step][:, i * LOCAL_ROWS : (i + 1) * LOCAL_ROWS] = pieces[chip, core]


def cut_tokens(spot, tokens):
    return pl.pallas_call(
        cut_kernel,
        in_specs=[SMEM, pl.BlockSpec(memory_space=pl.ANY)],
        out_shape=[jax.ShapeDtypeStruct((TOK_SUB, CHIP_ROWS), jnp.bfloat16)] * X,
        scratch_shapes=[
            pltpu.VMEM(tokens.shape, jnp.bfloat16),
            pltpu.VMEM((X, CORE, TOK_SUB, LOCAL_ROWS), jnp.bfloat16),
            pltpu.SemaphoreType.DMA(()),
        ],
        compiler_params=params(16),
        name="cut_tokens",
    )(spot, tokens)


def turn_kernel(*refs):
    out = refs[X]
    out[...] = jnp.concatenate([piece[...] for piece in refs[:X]], axis=0).T


def turn(pieces):
    return pl.pallas_call(
        turn_kernel,
        out_shape=jax.ShapeDtypeStruct((CHIP_ROWS, SHARD_K), jnp.bfloat16),
        compiler_params=params(16),
        name="turn",
    )(*pieces)


def gradient_kernel(spot, *refs):
    whole, halves, sources = refs[:7], refs[7:9], refs[9:13]
    mine, other, (left, right, tiles) = refs[13:17], refs[17], refs[18:]

    @pl.when(pl.program_id(0) == 0)
    def join_tokens():
        for j in range(7):
            left[:, j * SHARD_K : (j + 1) * SHARD_K] = whole[j][...]
        left[:LOCAL_ROWS, 7 * SHARD_K :] = halves[0][...]
        left[LOCAL_ROWS:, 7 * SHARD_K :] = halves[1][...]

    for j, step in enumerate((0, -1, 1, -2, 2, -3, 3, 4)):
        place = (spot[3] + step + N_TENSOR) % N_TENSOR
        for i in range(X):
            top = j * SHARD_K + i * TOK_SUB
            right[top : top + TOK_SUB] = sources[i][place]
    for column in range(WIDE):
        result = jnp.dot(
            left[...], right[:, column * BLOCK : (column + 1) * BLOCK],
            preferred_element_type=jnp.float32,
        ).astype(jnp.bfloat16)
        for side in range(CORE):
            for r in range(ROW_BLOCKS):
                for y in range(Y):
                    rows, cols = tile_of(y * ROW)
                    top = side * LOCAL_ROWS + r * STRIP + rows.start
                    tiles[side, y, column * ROW_BLOCKS + r] = result[top : top + TILE_ROWS, cols]
    for step in range(Y):
        place = (spot[0] + step) % Y
        mine[step][...] = tiles[0, place]
        other[step] = tiles[1, place]


def gradient_tiles(chunk, spot, lefts, near, far):
    resident = lambda a: pl.BlockSpec(a.shape, lambda c, spot: (0, 0))
    steps = COL_BLOCKS // 2 // WIDE
    blocks = WIDE * ROW_BLOCKS
    shape = (N_TENSOR, TOK_SUB, WIDE * BLOCK)
    near_spec = pl.BlockSpec(shape, lambda c, spot: (0, 0, steps * chunk + c))
    far_spec = pl.BlockSpec(shape, lambda c, spot: (0, 0, c))
    part = pl.BlockSpec((blocks, TILE_ROWS, TILE_COLS), lambda c, spot: (c, 0, 0))
    return pl.pallas_call(
        gradient_kernel,
        grid_spec=pltpu.PrefetchScalarGridSpec(
            num_scalar_prefetch=1,
            grid=(steps,),
            in_specs=[resident(a) for a in lefts] + [near_spec] * 3 + [far_spec],
            out_specs=[part] * Y
            + [pl.BlockSpec((Y, blocks, TILE_ROWS, TILE_COLS), lambda c, spot: (0, c, 0, 0))],
            scratch_shapes=[
                pltpu.VMEM((CHIP_ROWS, N_TENSOR * SHARD_K), jnp.bfloat16),
                pltpu.VMEM((N_TENSOR * SHARD_K, WIDE * BLOCK), jnp.bfloat16),
                pltpu.VMEM((CORE, Y, blocks, TILE_ROWS, TILE_COLS), jnp.bfloat16),
            ],
        ),
        out_shape=[jax.ShapeDtypeStruct((CHUNK_K, TILE_ROWS, TILE_COLS), jnp.bfloat16)] * Y
        + [jax.ShapeDtypeStruct((Y, CHUNK_K, TILE_ROWS, TILE_COLS), jnp.bfloat16)],
        compiler_params=params(30),
        cost_estimate=pl.CostEstimate(
            flops=2 * CHIP_ROWS * N_TENSOR * SHARD_K * 4 * BLOCK,
            bytes_accessed=8 * MIB, transcendentals=0,
        ),
        name="gradient_tiles",
    )(spot, *lefts, *near, far)


def add_cores_kernel(one, two, three, other, *outs):
    for d, (mine, out) in enumerate(zip((one, two, three), outs), 1):
        out[...] = (mine[...].astype(jnp.float32) + other[d].astype(jnp.float32)).astype(
            jnp.bfloat16
        )


def add_cores(parts, other):
    blocks = CHUNK_K // 4
    part = pl.BlockSpec((blocks, TILE_ROWS, TILE_COLS), lambda c: (c, 0, 0))
    return pl.pallas_call(
        add_cores_kernel,
        grid=(4,),
        in_specs=[part] * 3
        + [pl.BlockSpec((Y, blocks, TILE_ROWS, TILE_COLS), lambda c: (0, c, 0, 0))],
        out_specs=[part] * 3,
        out_shape=[jax.ShapeDtypeStruct(a.shape, a.dtype) for a in parts[1:]],
        compiler_params=params(16),
        name="add_cores",
    )(*parts[1:], other)


def to_slots_kernel(slot, *refs):
    out = refs[-1]
    out[...] = jnp.zeros_like(out)
    for chunk in range(2):
        mine, other, *rest = refs[5 * chunk : 5 * chunk + 5]

        def body(k, carry):
            total = mine[k].astype(jnp.float32) + other[0, k].astype(jnp.float32)
            for part in rest:
                total = total + part[k].astype(jnp.float32)
            out[slot[chunk * CHUNK_K + k]] = total.astype(jnp.bfloat16)
            return carry

        lax.fori_loop(0, CHUNK_K, body, 0, unroll=8)


def to_slots(slot, chunks):
    flat = [a for chunk in chunks for a in chunk]
    return pl.pallas_call(
        to_slots_kernel,
        in_specs=[SMEM] + [VMEM] * len(flat),
        out_shape=jax.ShapeDtypeStruct((N_DP * SLOTS, TILE_ROWS, TILE_COLS), jnp.bfloat16),
        compiler_params=params(16),
        name="to_slots",
    )(slot, *flat)


def from_slots_kernel(slot, tiles, out):
    def body(k, carry):
        out[k] = tiles[slot[k]]
        return carry

    lax.fori_loop(0, NBLK, body, 0, unroll=8)


def from_slots(slot, tiles):
    return pl.pallas_call(
        from_slots_kernel,
        in_specs=[SMEM, VMEM],
        out_shape=jax.ShapeDtypeStruct((NBLK, TILE_ROWS, TILE_COLS), jnp.bfloat16),
        compiler_params=params(16),
        name="from_slots",
    )(slot, tiles)


def assemble_kernel(tiles, out):
    for h in range(HOME):
        for m in range(N_DP):
            rows, cols = tile_of(m)
            out[0, h, rows, cols] = tiles[m, h]


def assemble(tiles):
    return pl.pallas_call(
        assemble_kernel,
        out_shape=jax.ShapeDtypeStruct((1, HOME, BLOCK, BLOCK), jnp.bfloat16),
        compiler_params=params(16),
        name="assemble",
    )(tiles)


def dot(a, b, ca, cb):
    return lax.dot_general(a, b, (((ca,), (cb,)), ((), ())), preferred_element_type=jnp.float32)


def update_kernel(
    live, tiles, basis_left, basis_right, first, second,
    update, grads, first_new, second_new,
):
    for s in range(SLOTS):
        for m in range(N_DP):
            rows, cols = tile_of(m)
            grads[s, rows, cols] = tiles[m, s]
        grad = grads[s]
        ql, qr = basis_left[0, s], basis_right[0, s]
        halfway = dot(ql, grad, 0, 0).astype(jnp.bfloat16)
        rotated = dot(halfway, qr, 1, 0)
        first_old, second_old = first[0, s], second[0, s]
        first_float = first_decay * first_old.astype(jnp.float32) + (1.0 - first_decay) * rotated
        second_float = (
            second_decay * second_old.astype(jnp.float32)
            + (1.0 - second_decay) * rotated * rotated
        )
        ratio = (first_float / (jnp.sqrt(second_float) + epsilon_value)).astype(jnp.bfloat16)
        turned = dot(ql, ratio, 1, 0).astype(jnp.bfloat16)
        result = dot(turned, qr, 1, 1).astype(jnp.bfloat16)
        for m in range(N_DP):
            rows, cols = tile_of(m)
            update[m, s] = result[rows, cols]
        alive = live[s] > 0
        first_new[0, s] = jnp.where(alive, first_float.astype(jnp.bfloat16), first_old)
        second_new[0, s] = jnp.where(alive, second_float.astype(jnp.bfloat16), second_old)


def update_blocks(live, tiles, basis_left, basis_right, first, second):
    like = lambda a: jax.ShapeDtypeStruct(a.shape, a.dtype)
    return pl.pallas_call(
        update_kernel,
        in_specs=[SMEM] + [VMEM] * 5,
        out_shape=[
            like(tiles),
            jax.ShapeDtypeStruct((SLOTS, BLOCK, BLOCK), jnp.bfloat16),
            like(first),
            like(second),
        ],
        compiler_params=params(63),
        name="update",
    )(live, tiles, basis_left, basis_right, first, second)


def factor_kernel(live, grads, left, right, left_new, right_new):
    alive = live[pl.program_id(0)] > 0
    grad = grads[0]
    scale = (1.0 - factor_decay) / BLOCK
    left_old, right_old = left[0, 0], right[0, 0]
    left_new[0, 0] = jnp.where(
        alive, factor_decay * left_old + scale * dot(grad, grad, 1, 1), left_old
    )
    right_new[0, 0] = jnp.where(
        alive, factor_decay * right_old + scale * dot(grad, grad, 0, 0), right_old
    )


def update_factors(live, grads, left, right):
    state = pl.BlockSpec((1, 1, BLOCK, BLOCK), lambda s, live: (0, s, 0, 0))
    return pl.pallas_call(
        factor_kernel,
        grid_spec=pltpu.PrefetchScalarGridSpec(
            num_scalar_prefetch=1,
            grid=(SLOTS,),
            in_specs=[pl.BlockSpec((1, BLOCK, BLOCK), lambda s, live: (s, 0, 0))] + [state] * 2,
            out_specs=[state] * 2,
        ),
        out_shape=[jax.ShapeDtypeStruct(a.shape, a.dtype) for a in (left, right)],
        compiler_params=params(32),
        cost_estimate=pl.CostEstimate(
            flops=4 * SLOTS * BLOCK**3, bytes_accessed=6 * MIB, transcendentals=0
        ),
        name="factors",
    )(live, grads, left, right)


def spread(array, axes):
    return lax.all_to_all(array, axes, split_axis=0, concat_axis=0, tiled=True)


def ring(size, step):
    return [(i, (i + step) % size) for i in range(size)]


def gather_row(spot, tokens, grads):
    up, down = ring(N_TENSOR, 1), ring(N_TENSOR, -1)
    ahead, back = ring(X, 1), ring(X, -1)

    cut = cut_tokens(spot, tokens)
    pieces = [cut[0]] + [lax.ppermute(cut[step], "x", ring(X, step)) for step in (1, 3, 2)]
    pieces, grads = lax.optimization_barrier((pieces, grads))
    behind, before = lax.ppermute(grads, "x", ahead), lax.ppermute(grads, "x", back)
    mine = turn(pieces)
    below, above = lax.ppermute(mine, "z", up), lax.ppermute(mine, "z", down)
    whole = [mine, below, above]
    below, above = lax.ppermute(below, "z", up), lax.ppermute(above, "z", down)
    whole += [below, above]
    behind, before, below, above = lax.optimization_barrier((behind, before, below, above))
    half = grads.shape[-1] // 2
    far = [
        lax.ppermute(behind[..., :half], "x", ahead),
        lax.ppermute(before[..., half:], "x", back),
    ]
    below, above = lax.ppermute(below, "z", up), lax.ppermute(above, "z", down)
    whole += [below, above]
    halves = [
        lax.ppermute(below[:LOCAL_ROWS], "z", up),
        lax.ppermute(above[LOCAL_ROWS:], "z", down),
    ]
    return whole + halves, [grads, behind, before], far


def sum_parts(parts):
    mine, other = parts[:Y], lax.ppermute(parts[Y], "core", ring(CORE, 1))
    one, two, three = add_cores(mine, other)
    moved = [
        lax.ppermute(a, "y", ring(Y, step)) for a, step in ((two, 2), (one, 1), (three, 3))
    ]
    return [mine[0], other] + moved


def local(
    tokens, grad_out, owner, left_factor, right_factor,
    left_basis, right_basis, first_moment, second_moment,
):
    owner_row = owner[0]
    block_ids = jnp.arange(NBLK, dtype=jnp.int32)
    same = owner_row[:, None] == owner_row[None, :]
    before = block_ids[None, :] < block_ids[:, None]
    rank = jnp.sum((same & before).astype(jnp.int32), axis=1)
    slot = owner_row * SLOTS + rank
    held = jnp.sum((owner_row == lax.axis_index(DP)).astype(jnp.int32))
    live = (jnp.arange(SLOTS, dtype=jnp.int32) < held).astype(jnp.int32)

    spot = jnp.stack([lax.axis_index(axis) for axis in (*DP, "z")]).astype(jnp.int32)
    grads = grad_out.reshape(N_TENSOR, TOK_SUB, grad_out.shape[1])
    lefts, near, far = gather_row(spot, tokens, grads)
    chunks = [
        sum_parts(gradient_tiles(chunk, spot, lefts, near, far[chunk])) for chunk in range(2)
    ]
    tiles = to_slots(slot, chunks).reshape(N_DP, SLOTS, TILE_ROWS, TILE_COLS)
    update, grad_blocks, first_new, second_new = update_blocks(
        live, spread(tiles, DP), left_basis, right_basis, first_moment, second_moment
    )
    left_new, right_new = update_factors(live, grad_blocks, left_factor, right_factor)
    back = spread(update, DP).reshape(N_DP * SLOTS, TILE_ROWS, TILE_COLS)
    picked = from_slots(slot, back).reshape(N_DP, HOME, TILE_ROWS, TILE_COLS)
    home_update = assemble(spread(picked, DP))
    return (home_update, left_new, right_new, first_new, second_new)


def solution(mesh):
    split = Mesh(mesh.devices.reshape(Y, X, CORE, N_TENSOR), ("y", "x", "core", "z"))
    state = P("z", DP, None, None)
    return jax.shard_map(
        local,
        mesh=split,
        in_specs=(P((*DP, "z"), None), P(DP, "z"), P("z", None)) + (state,) * 6,
        out_specs=(state,) * 5,
        check_vma=False,
    )
```

```python
import jax
import jax.numpy as jnp
from jax import lax
from jax.experimental import pallas as pl
from jax.experimental.pallas import tpu as pltpu
from jax.sharding import Mesh
from jax.sharding import PartitionSpec as P

BLOCK = 256
TILE_ROWS = 16
TILE_COLS = 128
Y, X, CORE = 4, 4, 2
N_DP = Y * X * CORE
N_TENSOR = 8
ROW = X * CORE
STRIP = BLOCK // ROW
SLOTS = 5
HOME = 4
NBLK = 128
ROW_BLOCKS = 16
COL_BLOCKS = 8
TOK_SUB = 32
LOCAL_ROWS = ROW_BLOCKS * STRIP
DP = ("y", "x", "core")
CHIP_ROWS = LOCAL_ROWS * CORE
SHARD_K = X * TOK_SUB
WIDE = 2
CHUNK_K = NBLK // 2

factor_decay = 0.9
first_decay = 0.95
second_decay = 0.95
epsilon_value = 1e-08

MIB = 1024 * 1024
SMEM = pl.BlockSpec(memory_space=pltpu.SMEM)
VMEM = pl.BlockSpec(memory_space=pltpu.VMEM)


def params(mib):
    return pltpu.CompilerParams(vmem_limit_bytes=mib * MIB)


def tile_of(m):
    y, strip = m // ROW, m % ROW
    top, side = STRIP * strip + TILE_ROWS * (y // 2), TILE_COLS * (y % 2)
    return slice(top, top + TILE_ROWS), slice(side, side + TILE_COLS)


def cut_kernel(spot, tokens, *refs):
    outs, (held, pieces, sem) = refs[:X], refs[X:]
    copy = pltpu.make_async_copy(tokens, held, sem)
    copy.start()
    copy.wait()
    for strip in range(ROW):
        pieces[strip // CORE, strip % CORE] = jnp.concatenate(
            [
                held[:, r * BLOCK + STRIP * strip : r * BLOCK + STRIP * (strip + 1)]
                for r in range(ROW_BLOCKS)
            ],
            axis=1,
        )
    for step in range(X):
        chip = (spot[1] + step) % X
        for i in range(CORE):
            core = (spot[2] + i) % CORE
            outs[step][:, i * LOCAL_ROWS : (i + 1) * LOCAL_ROWS] = pieces[chip, core]


def cut_tokens(spot, tokens):
    return pl.pallas_call(
        cut_kernel,
        in_specs=[SMEM, pl.BlockSpec(memory_space=pl.ANY)],
        out_shape=[jax.ShapeDtypeStruct((TOK_SUB, CHIP_ROWS), jnp.bfloat16)] * X,
        scratch_shapes=[
            pltpu.VMEM(tokens.shape, jnp.bfloat16),
            pltpu.VMEM((X, CORE, TOK_SUB, LOCAL_ROWS), jnp.bfloat16),
            pltpu.SemaphoreType.DMA(()),
        ],
        compiler_params=params(16),
        name="cut_tokens",
    )(spot, tokens)


def turn_kernel(*refs):
    out = refs[X]
    out[...] = jnp.concatenate([piece[...] for piece in refs[:X]], axis=0).T


def turn(pieces):
    return pl.pallas_call(
        turn_kernel,
        out_shape=jax.ShapeDtypeStruct((CHIP_ROWS, SHARD_K), jnp.bfloat16),
        compiler_params=params(16),
        name="turn",
    )(*pieces)


def gradient_kernel(spot, *refs):
    whole, halves, sources = refs[:7], refs[7:9], refs[9:13]
    mine, other, (left, right, tiles) = refs[13:17], refs[17], refs[18:]

    @pl.when(pl.program_id(0) == 0)
    def join_tokens():
        for j in range(7):
            left[:, j * SHARD_K : (j + 1) * SHARD_K] = whole[j][...]
        left[:LOCAL_ROWS, 7 * SHARD_K :] = halves[0][...]
        left[LOCAL_ROWS:, 7 * SHARD_K :] = halves[1][...]

    for j, step in enumerate((0, -1, 1, -2, 2, -3, 3, 4)):
        place = (spot[3] + step + N_TENSOR) % N_TENSOR
        for i in range(X):
            top = j * SHARD_K + i * TOK_SUB
            right[top : top + TOK_SUB] = sources[i][place]
    for column in range(WIDE):
        result = jnp.dot(
            left[...], right[:, column * BLOCK : (column + 1) * BLOCK],
            preferred_element_type=jnp.float32,
        ).astype(jnp.bfloat16)
        for side in range(CORE):
            for r in range(ROW_BLOCKS):
                for y in range(Y):
                    rows, cols = tile_of(y * ROW)
                    top = side * LOCAL_ROWS + r * STRIP + rows.start
                    tiles[side, y, column * ROW_BLOCKS + r] = result[top : top + TILE_ROWS, cols]
    for step in range(Y):
        place = (spot[0] + step) % Y
        mine[step][...] = tiles[0, place]
        other[step] = tiles[1, place]


def gradient_tiles(chunk, spot, lefts, near, far):
    resident = lambda a: pl.BlockSpec(a.shape, lambda c, spot: (0, 0))
    steps = COL_BLOCKS // 2 // WIDE
    blocks = WIDE * ROW_BLOCKS
    shape = (N_TENSOR, TOK_SUB, WIDE * BLOCK)
    near_spec = pl.BlockSpec(shape, lambda c, spot: (0, 0, steps * chunk + c))
    far_spec = pl.BlockSpec(shape, lambda c, spot: (0, 0, c))
    part = pl.BlockSpec((blocks, TILE_ROWS, TILE_COLS), lambda c, spot: (c, 0, 0))
    return pl.pallas_call(
        gradient_kernel,
        grid_spec=pltpu.PrefetchScalarGridSpec(
            num_scalar_prefetch=1,
            grid=(steps,),
            in_specs=[resident(a) for a in lefts] + [near_spec] * 3 + [far_spec],
            out_specs=[part] * Y
            + [pl.BlockSpec((Y, blocks, TILE_ROWS, TILE_COLS), lambda c, spot: (0, c, 0, 0))],
            scratch_shapes=[
                pltpu.VMEM((CHIP_ROWS, N_TENSOR * SHARD_K), jnp.bfloat16),
                pltpu.VMEM((N_TENSOR * SHARD_K, WIDE * BLOCK), jnp.bfloat16),
                pltpu.VMEM((CORE, Y, blocks, TILE_ROWS, TILE_COLS), jnp.bfloat16),
            ],
        ),
        out_shape=[jax.ShapeDtypeStruct((CHUNK_K, TILE_ROWS, TILE_COLS), jnp.bfloat16)] * Y
        + [jax.ShapeDtypeStruct((Y, CHUNK_K, TILE_ROWS, TILE_COLS), jnp.bfloat16)],
        compiler_params=params(30),
        cost_estimate=pl.CostEstimate(
            flops=2 * CHIP_ROWS * N_TENSOR * SHARD_K * 4 * BLOCK,
            bytes_accessed=8 * MIB, transcendentals=0,
        ),
        name="gradient_tiles",
    )(spot, *lefts, *near, far)


def add_cores_kernel(one, two, three, other, *outs):
    for d, (mine, out) in enumerate(zip((one, two, three), outs), 1):
        out[...] = (mine[...].astype(jnp.float32) + other[d].astype(jnp.float32)).astype(
            jnp.bfloat16
        )


def add_cores(parts, other):
    blocks = CHUNK_K // 4
    part = pl.BlockSpec((blocks, TILE_ROWS, TILE_COLS), lambda c: (c, 0, 0))
    return pl.pallas_call(
        add_cores_kernel,
        grid=(4,),
        in_specs=[part] * 3
        + [pl.BlockSpec((Y, blocks, TILE_ROWS, TILE_COLS), lambda c: (0, c, 0, 0))],
        out_specs=[part] * 3,
        out_shape=[jax.ShapeDtypeStruct(a.shape, a.dtype) for a in parts[1:]],
        compiler_params=params(16),
        name="add_cores",
    )(*parts[1:], other)


def sum_kernel(mine, other, one, two, three, out):
    total = mine[...].astype(jnp.float32) + other[0].astype(jnp.float32)
    for part in (one, two, three):
        total = total + part[...].astype(jnp.float32)
    out[...] = total.astype(jnp.bfloat16)


def sum_chunk(parts):
    blocks = CHUNK_K // 4
    part = pl.BlockSpec((blocks, TILE_ROWS, TILE_COLS), lambda c: (c, 0, 0))
    first = pl.BlockSpec((1, blocks, TILE_ROWS, TILE_COLS), lambda c: (0, c, 0, 0))
    return pl.pallas_call(
        sum_kernel,
        grid=(4,),
        in_specs=[part, first, part, part, part],
        out_specs=part,
        out_shape=jax.ShapeDtypeStruct((CHUNK_K, TILE_ROWS, TILE_COLS), jnp.bfloat16),
        compiler_params=params(16),
        cost_estimate=pl.CostEstimate(flops=MIB, bytes_accessed=2 * MIB, transcendentals=0),
        name="sum_chunk",
    )(*parts)


def to_slots_kernel(slot, summed, mine, other, one, two, three, out):
    out[...] = jnp.zeros_like(out)

    def early(k, carry):
        out[slot[k]] = summed[k]
        return carry

    def late(k, carry):
        total = mine[k].astype(jnp.float32) + other[0, k].astype(jnp.float32)
        for part in (one, two, three):
            total = total + part[k].astype(jnp.float32)
        out[slot[CHUNK_K + k]] = total.astype(jnp.bfloat16)
        return carry

    lax.fori_loop(0, CHUNK_K, early, 0, unroll=8)
    lax.fori_loop(0, CHUNK_K, late, 0, unroll=8)


def to_slots(slot, chunks):
    return pl.pallas_call(
        to_slots_kernel,
        in_specs=[SMEM] + [VMEM] * 6,
        out_shape=jax.ShapeDtypeStruct((N_DP * SLOTS, TILE_ROWS, TILE_COLS), jnp.bfloat16),
        compiler_params=params(16),
        name="to_slots",
    )(slot, sum_chunk(chunks[0]), *chunks[1])


def from_slots_kernel(slot, tiles, out):
    def body(k, carry):
        out[k] = tiles[slot[k]]
        return carry

    lax.fori_loop(0, NBLK, body, 0, unroll=8)


def from_slots(slot, tiles):
    return pl.pallas_call(
        from_slots_kernel,
        in_specs=[SMEM, VMEM],
        out_shape=jax.ShapeDtypeStruct((NBLK, TILE_ROWS, TILE_COLS), jnp.bfloat16),
        compiler_params=params(16),
        name="from_slots",
    )(slot, tiles)


def assemble_kernel(tiles, out):
    for h in range(HOME):
        for m in range(N_DP):
            rows, cols = tile_of(m)
            out[0, h, rows, cols] = tiles[m, h]


def assemble(tiles):
    return pl.pallas_call(
        assemble_kernel,
        out_shape=jax.ShapeDtypeStruct((1, HOME, BLOCK, BLOCK), jnp.bfloat16),
        compiler_params=params(16),
        name="assemble",
    )(tiles)


def dot(a, b, ca, cb):
    return lax.dot_general(a, b, (((ca,), (cb,)), ((), ())), preferred_element_type=jnp.float32)


def update_kernel(
    live, tiles, basis_left, basis_right, first, second,
    update, grads, first_new, second_new,
):
    for s in range(SLOTS):
        for m in range(N_DP):
            rows, cols = tile_of(m)
            grads[s, rows, cols] = tiles[m, s]
        grad = grads[s]
        ql, qr = basis_left[0, s], basis_right[0, s]
        halfway = dot(ql, grad, 0, 0).astype(jnp.bfloat16)
        rotated = dot(halfway, qr, 1, 0)
        first_old, second_old = first[0, s], second[0, s]
        first_float = first_decay * first_old.astype(jnp.float32) + (1.0 - first_decay) * rotated
        second_float = (
            second_decay * second_old.astype(jnp.float32)
            + (1.0 - second_decay) * rotated * rotated
        )
        ratio = (first_float / (jnp.sqrt(second_float) + epsilon_value)).astype(jnp.bfloat16)
        turned = dot(ql, ratio, 1, 0).astype(jnp.bfloat16)
        result = dot(turned, qr, 1, 1).astype(jnp.bfloat16)
        for m in range(N_DP):
            rows, cols = tile_of(m)
            update[m, s] = result[rows, cols]
        alive = live[s] > 0
        first_new[0, s] = jnp.where(alive, first_float.astype(jnp.bfloat16), first_old)
        second_new[0, s] = jnp.where(alive, second_float.astype(jnp.bfloat16), second_old)


def update_blocks(live, tiles, basis_left, basis_right, first, second):
    like = lambda a: jax.ShapeDtypeStruct(a.shape, a.dtype)
    return pl.pallas_call(
        update_kernel,
        in_specs=[SMEM] + [VMEM] * 5,
        out_shape=[
            like(tiles),
            jax.ShapeDtypeStruct((SLOTS, BLOCK, BLOCK), jnp.bfloat16),
            like(first),
            like(second),
        ],
        compiler_params=params(52),
        name="update",
    )(live, tiles, basis_left, basis_right, first, second)


def factor_kernel(live, grads, left, right, left_new, right_new):
    alive = live[pl.program_id(0)] > 0
    grad = grads[0]
    scale = (1.0 - factor_decay) / BLOCK
    left_old, right_old = left[0, 0], right[0, 0]
    left_new[0, 0] = jnp.where(
        alive, factor_decay * left_old + scale * dot(grad, grad, 1, 1), left_old
    )
    right_new[0, 0] = jnp.where(
        alive, factor_decay * right_old + scale * dot(grad, grad, 0, 0), right_old
    )


def update_factors(live, grads, left, right):
    state = pl.BlockSpec((1, 1, BLOCK, BLOCK), lambda s, live: (0, s, 0, 0))
    return pl.pallas_call(
        factor_kernel,
        grid_spec=pltpu.PrefetchScalarGridSpec(
            num_scalar_prefetch=1,
            grid=(SLOTS,),
            in_specs=[pl.BlockSpec((1, BLOCK, BLOCK), lambda s, live: (s, 0, 0))] + [state] * 2,
            out_specs=[state] * 2,
        ),
        out_shape=[jax.ShapeDtypeStruct(a.shape, a.dtype) for a in (left, right)],
        compiler_params=params(32),
        cost_estimate=pl.CostEstimate(
            flops=4 * SLOTS * BLOCK**3, bytes_accessed=6 * MIB, transcendentals=0
        ),
        name="factors",
    )(live, grads, left, right)


def spread(array, axes):
    return lax.all_to_all(array, axes, split_axis=0, concat_axis=0, tiled=True)


def ring(size, step):
    return [(i, (i + step) % size) for i in range(size)]


def gather_row(spot, tokens, grads):
    up, down = ring(N_TENSOR, 1), ring(N_TENSOR, -1)
    ahead, back = ring(X, 1), ring(X, -1)

    cut = cut_tokens(spot, tokens)
    pieces = [cut[0]] + [lax.ppermute(cut[step], "x", ring(X, step)) for step in (1, 3, 2)]
    pieces, grads = lax.optimization_barrier((pieces, grads))
    behind, before = lax.ppermute(grads, "x", ahead), lax.ppermute(grads, "x", back)
    mine = turn(pieces)
    below, above = lax.ppermute(mine, "z", up), lax.ppermute(mine, "z", down)
    whole = [mine, below, above]
    below, above = lax.ppermute(below, "z", up), lax.ppermute(above, "z", down)
    whole += [below, above]
    below, above = lax.ppermute(below, "z", up), lax.ppermute(above, "z", down)
    whole += [below, above]
    behind, before, below, above = lax.optimization_barrier((behind, before, below, above))
    half = grads.shape[-1] // 2
    far = [
        lax.ppermute(behind[..., :half], "x", ahead),
        lax.ppermute(before[..., half:], "x", back),
    ]
    halves = [
        lax.ppermute(below[:LOCAL_ROWS], "z", up),
        lax.ppermute(above[LOCAL_ROWS:], "z", down),
    ]
    return whole + halves, [grads, behind, before], far


def sum_parts(parts):
    mine, other = parts[:Y], lax.ppermute(parts[Y], "core", ring(CORE, 1))
    one, two, three = add_cores(mine, other)
    moved = [
        lax.ppermute(a, "y", ring(Y, step)) for a, step in ((one, 1), (two, 2), (three, 3))
    ]
    return [mine[0], other] + moved


def local(
    tokens, grad_out, owner, left_factor, right_factor,
    left_basis, right_basis, first_moment, second_moment,
):
    owner_row = owner[0]
    block_ids = jnp.arange(NBLK, dtype=jnp.int32)
    same = owner_row[:, None] == owner_row[None, :]
    before = block_ids[None, :] < block_ids[:, None]
    rank = jnp.sum((same & before).astype(jnp.int32), axis=1)
    slot = owner_row * SLOTS + rank
    held = jnp.sum((owner_row == lax.axis_index(DP)).astype(jnp.int32))
    live = (jnp.arange(SLOTS, dtype=jnp.int32) < held).astype(jnp.int32)

    spot = jnp.stack([lax.axis_index(axis) for axis in (*DP, "z")]).astype(jnp.int32)
    grads = grad_out.reshape(N_TENSOR, TOK_SUB, grad_out.shape[1])
    lefts, near, far = gather_row(spot, tokens, grads)
    chunks = [
        sum_parts(gradient_tiles(chunk, spot, lefts, near, far[chunk])) for chunk in range(2)
    ]
    tiles = to_slots(slot, chunks).reshape(N_DP, SLOTS, TILE_ROWS, TILE_COLS)
    update, grad_blocks, first_new, second_new = update_blocks(
        live, spread(tiles, DP), left_basis, right_basis, first_moment, second_moment
    )
    left_new, right_new = update_factors(live, grad_blocks, left_factor, right_factor)
    back = spread(update, DP).reshape(N_DP * SLOTS, TILE_ROWS, TILE_COLS)
    picked = from_slots(slot, back).reshape(N_DP, HOME, TILE_ROWS, TILE_COLS)
    home_update = assemble(spread(picked, DP))
    return (home_update, left_new, right_new, first_new, second_new)


def solution(mesh):
    split = Mesh(mesh.devices.reshape(Y, X, CORE, N_TENSOR), ("y", "x", "core", "z"))
    state = P("z", DP, None, None)
    return jax.shard_map(
        local,
        mesh=split,
        in_specs=(P((*DP, "z"), None), P(DP, "z"), P("z", None)) + (state,) * 6,
        out_specs=(state,) * 5,
        check_vma=False,
    )
```

```python
import jax
import jax.numpy as jnp
from jax import lax
from jax.experimental import pallas as pl
from jax.experimental.pallas import tpu as pltpu
from jax.sharding import Mesh
from jax.sharding import PartitionSpec as P

BLOCK = 256
TILE_ROWS = 16
TILE_COLS = 128
Y, X, CORE = 4, 4, 2
N_DP = Y * X * CORE
N_TENSOR = 8
ROW = X * CORE
STRIP = BLOCK // ROW
SLOTS = 5
HOME = 4
NBLK = 128
ROW_BLOCKS = 16
COL_BLOCKS = 8
TOK_SUB = 32
LOCAL_ROWS = ROW_BLOCKS * STRIP
DP = ("y", "x", "core")
CHIP_ROWS = LOCAL_ROWS * CORE
SHARD_K = X * TOK_SUB
WIDE = 2
CHUNK_K = NBLK // 2

factor_decay = 0.9
first_decay = 0.95
second_decay = 0.95
epsilon_value = 1e-08

MIB = 1024 * 1024
SMEM = pl.BlockSpec(memory_space=pltpu.SMEM)
VMEM = pl.BlockSpec(memory_space=pltpu.VMEM)


def params(mib):
    return pltpu.CompilerParams(vmem_limit_bytes=mib * MIB)


def tile_of(m):
    y, strip = m // ROW, m % ROW
    top, side = STRIP * strip + TILE_ROWS * (y // 2), TILE_COLS * (y % 2)
    return slice(top, top + TILE_ROWS), slice(side, side + TILE_COLS)


def cut_kernel(spot, tokens, *refs):
    outs, (held, pieces, sem) = refs[:X], refs[X:]
    copy = pltpu.make_async_copy(tokens, held, sem)
    copy.start()
    copy.wait()
    for strip in range(ROW):
        pieces[strip // CORE, strip % CORE] = jnp.concatenate(
            [
                held[:, r * BLOCK + STRIP * strip : r * BLOCK + STRIP * (strip + 1)]
                for r in range(ROW_BLOCKS)
            ],
            axis=1,
        )
    for step in range(X):
        chip = (spot[1] + step) % X
        for i in range(CORE):
            core = (spot[2] + i) % CORE
            outs[step][:, i * LOCAL_ROWS : (i + 1) * LOCAL_ROWS] = pieces[chip, core]


def cut_tokens(spot, tokens):
    return pl.pallas_call(
        cut_kernel,
        in_specs=[SMEM, pl.BlockSpec(memory_space=pl.ANY)],
        out_shape=[jax.ShapeDtypeStruct((TOK_SUB, CHIP_ROWS), jnp.bfloat16)] * X,
        scratch_shapes=[
            pltpu.VMEM(tokens.shape, jnp.bfloat16),
            pltpu.VMEM((X, CORE, TOK_SUB, LOCAL_ROWS), jnp.bfloat16),
            pltpu.SemaphoreType.DMA(()),
        ],
        compiler_params=params(16),
        name="cut_tokens",
    )(spot, tokens)


def turn_kernel(*refs):
    out = refs[X]
    out[...] = jnp.concatenate([piece[...] for piece in refs[:X]], axis=0).T


def turn(pieces):
    return pl.pallas_call(
        turn_kernel,
        out_shape=jax.ShapeDtypeStruct((CHIP_ROWS, SHARD_K), jnp.bfloat16),
        compiler_params=params(16),
        name="turn",
    )(*pieces)


def gradient_kernel(spot, *refs):
    whole, halves, sources = refs[:7], refs[7:9], refs[9:13]
    mine, other, (left, right, tiles) = refs[13:17], refs[17], refs[18:]

    @pl.when(pl.program_id(0) == 0)
    def join_tokens():
        for j in range(7):
            left[:, j * SHARD_K : (j + 1) * SHARD_K] = whole[j][...]
        left[:LOCAL_ROWS, 7 * SHARD_K :] = halves[0][...]
        left[LOCAL_ROWS:, 7 * SHARD_K :] = halves[1][...]

    for j, step in enumerate((0, -1, 1, -2, 2, -3, 3, 4)):
        place = (spot[3] + step + N_TENSOR) % N_TENSOR
        for i in range(X):
            top = j * SHARD_K + i * TOK_SUB
            right[top : top + TOK_SUB] = sources[i][place]
    for column in range(WIDE):
        result = jnp.dot(
            left[...], right[:, column * BLOCK : (column + 1) * BLOCK],
            preferred_element_type=jnp.float32,
        ).astype(jnp.bfloat16)
        for side in range(CORE):
            for r in range(ROW_BLOCKS):
                for y in range(Y):
                    rows, cols = tile_of(y * ROW)
                    top = side * LOCAL_ROWS + r * STRIP + rows.start
                    tiles[side, y, column * ROW_BLOCKS + r] = result[top : top + TILE_ROWS, cols]
    for step in range(Y):
        place = (spot[0] + step) % Y
        mine[step][...] = tiles[0, place]
        other[step] = tiles[1, place]


def gradient_tiles(chunk, spot, lefts, near, far):
    resident = lambda a: pl.BlockSpec(a.shape, lambda c, spot: (0, 0))
    steps = COL_BLOCKS // 2 // WIDE
    blocks = WIDE * ROW_BLOCKS
    shape = (N_TENSOR, TOK_SUB, WIDE * BLOCK)
    near_spec = pl.BlockSpec(shape, lambda c, spot: (0, 0, steps * chunk + c))
    far_spec = pl.BlockSpec(shape, lambda c, spot: (0, 0, c))
    part = pl.BlockSpec((blocks, TILE_ROWS, TILE_COLS), lambda c, spot: (c, 0, 0))
    return pl.pallas_call(
        gradient_kernel,
        grid_spec=pltpu.PrefetchScalarGridSpec(
            num_scalar_prefetch=1,
            grid=(steps,),
            in_specs=[resident(a) for a in lefts] + [near_spec] * 3 + [far_spec],
            out_specs=[part] * Y
            + [pl.BlockSpec((Y, blocks, TILE_ROWS, TILE_COLS), lambda c, spot: (0, c, 0, 0))],
            scratch_shapes=[
                pltpu.VMEM((CHIP_ROWS, N_TENSOR * SHARD_K), jnp.bfloat16),
                pltpu.VMEM((N_TENSOR * SHARD_K, WIDE * BLOCK), jnp.bfloat16),
                pltpu.VMEM((CORE, Y, blocks, TILE_ROWS, TILE_COLS), jnp.bfloat16),
            ],
        ),
        out_shape=[jax.ShapeDtypeStruct((CHUNK_K, TILE_ROWS, TILE_COLS), jnp.bfloat16)] * Y
        + [jax.ShapeDtypeStruct((Y, CHUNK_K, TILE_ROWS, TILE_COLS), jnp.bfloat16)],
        compiler_params=params(30),
        cost_estimate=pl.CostEstimate(
            flops=2 * CHIP_ROWS * N_TENSOR * SHARD_K * 4 * BLOCK,
            bytes_accessed=8 * MIB, transcendentals=0,
        ),
        name="gradient_tiles",
    )(spot, *lefts, *near, far)


def add_cores_kernel(one, two, three, other, *outs):
    for d, (mine, out) in enumerate(zip((one, two, three), outs), 1):
        out[...] = (mine[...].astype(jnp.float32) + other[d].astype(jnp.float32)).astype(
            jnp.bfloat16
        )


def add_cores(parts, other):
    return pl.pallas_call(
        add_cores_kernel,
        out_shape=[jax.ShapeDtypeStruct(a.shape, a.dtype) for a in parts[1:]],
        compiler_params=params(16),
        name="add_cores",
    )(*parts[1:], other)


def sum_kernel(mine, other, one, two, three, out):
    total = mine[...].astype(jnp.float32) + other[0].astype(jnp.float32)
    for part in (one, two, three):
        total = total + part[...].astype(jnp.float32)
    out[...] = total.astype(jnp.bfloat16)


def sum_chunk(parts):
    return pl.pallas_call(
        sum_kernel,
        out_shape=jax.ShapeDtypeStruct((CHUNK_K, TILE_ROWS, TILE_COLS), jnp.bfloat16),
        compiler_params=params(16),
        cost_estimate=pl.CostEstimate(flops=MIB, bytes_accessed=2 * MIB, transcendentals=0),
        name="sum_chunk",
    )(*parts)


def to_slots_kernel(slot, summed, mine, other, one, two, three, out):
    out[...] = jnp.zeros_like(out)

    def early(k, carry):
        out[slot[k]] = summed[k]
        return carry

    def late(k, carry):
        total = mine[k].astype(jnp.float32) + other[0, k].astype(jnp.float32)
        for part in (one, two, three):
            total = total + part[k].astype(jnp.float32)
        out[slot[CHUNK_K + k]] = total.astype(jnp.bfloat16)
        return carry

    lax.fori_loop(0, CHUNK_K, early, 0, unroll=16)
    lax.fori_loop(0, CHUNK_K, late, 0, unroll=16)


def to_slots(slot, chunks):
    return pl.pallas_call(
        to_slots_kernel,
        in_specs=[SMEM] + [VMEM] * 6,
        out_shape=jax.ShapeDtypeStruct((N_DP * SLOTS, TILE_ROWS, TILE_COLS), jnp.bfloat16),
        compiler_params=params(16),
        name="to_slots",
    )(slot, sum_chunk(chunks[0]), *chunks[1])


def from_slots_kernel(slot, tiles, out):
    def body(k, carry):
        out[k] = tiles[slot[k]]
        return carry

    lax.fori_loop(0, NBLK, body, 0, unroll=32)


def from_slots(slot, tiles):
    return pl.pallas_call(
        from_slots_kernel,
        in_specs=[SMEM, VMEM],
        out_shape=jax.ShapeDtypeStruct((NBLK, TILE_ROWS, TILE_COLS), jnp.bfloat16),
        compiler_params=params(16),
        name="from_slots",
    )(slot, tiles)


def assemble_kernel(tiles, out):
    for h in range(HOME):
        for m in range(N_DP):
            rows, cols = tile_of(m)
            out[0, h, rows, cols] = tiles[m, h]


def assemble(tiles):
    return pl.pallas_call(
        assemble_kernel,
        out_shape=jax.ShapeDtypeStruct((1, HOME, BLOCK, BLOCK), jnp.bfloat16),
        compiler_params=params(16),
        name="assemble",
    )(tiles)


def dot(a, b, ca, cb):
    return lax.dot_general(a, b, (((ca,), (cb,)), ((), ())), preferred_element_type=jnp.float32)


def update_kernel(
    live, tiles, basis_left, basis_right, first, second,
    update, grads, first_new, second_new,
):
    for s in range(SLOTS):
        for m in range(N_DP):
            rows, cols = tile_of(m)
            grads[s, rows, cols] = tiles[m, s]
        grad = grads[s]
        ql, qr = basis_left[0, s], basis_right[0, s]
        halfway = dot(ql, grad, 0, 0).astype(jnp.bfloat16)
        rotated = dot(halfway, qr, 1, 0)
        first_old, second_old = first[0, s], second[0, s]
        first_float = first_decay * first_old.astype(jnp.float32) + (1.0 - first_decay) * rotated
        second_float = (
            second_decay * second_old.astype(jnp.float32)
            + (1.0 - second_decay) * rotated * rotated
        )
        ratio = (first_float / (jnp.sqrt(second_float) + epsilon_value)).astype(jnp.bfloat16)
        turned = dot(ql, ratio, 1, 0).astype(jnp.bfloat16)
        result = dot(turned, qr, 1, 1).astype(jnp.bfloat16)
        for m in range(N_DP):
            rows, cols = tile_of(m)
            update[m, s] = result[rows, cols]
        alive = live[s] > 0
        first_new[0, s] = jnp.where(alive, first_float.astype(jnp.bfloat16), first_old)
        second_new[0, s] = jnp.where(alive, second_float.astype(jnp.bfloat16), second_old)


def update_blocks(live, tiles, basis_left, basis_right, first, second):
    like = lambda a: jax.ShapeDtypeStruct(a.shape, a.dtype)
    return pl.pallas_call(
        update_kernel,
        in_specs=[SMEM] + [VMEM] * 5,
        out_shape=[
            like(tiles),
            jax.ShapeDtypeStruct((SLOTS, BLOCK, BLOCK), jnp.bfloat16),
            like(first),
            like(second),
        ],
        compiler_params=params(52),
        name="update",
    )(live, tiles, basis_left, basis_right, first, second)


def factor_kernel(live, grads, left, right, left_new, right_new):
    alive = live[pl.program_id(0)] > 0
    grad = grads[0]
    scale = (1.0 - factor_decay) / BLOCK
    left_old, right_old = left[0, 0], right[0, 0]
    left_new[0, 0] = jnp.where(
        alive, factor_decay * left_old + scale * dot(grad, grad, 1, 1), left_old
    )
    right_new[0, 0] = jnp.where(
        alive, factor_decay * right_old + scale * dot(grad, grad, 0, 0), right_old
    )


def update_factors(live, grads, left, right):
    state = pl.BlockSpec((1, 1, BLOCK, BLOCK), lambda s, live: (0, s, 0, 0))
    return pl.pallas_call(
        factor_kernel,
        grid_spec=pltpu.PrefetchScalarGridSpec(
            num_scalar_prefetch=1,
            grid=(SLOTS,),
            in_specs=[pl.BlockSpec((1, BLOCK, BLOCK), lambda s, live: (s, 0, 0))] + [state] * 2,
            out_specs=[state] * 2,
        ),
        out_shape=[jax.ShapeDtypeStruct(a.shape, a.dtype) for a in (left, right)],
        compiler_params=params(32),
        cost_estimate=pl.CostEstimate(
            flops=4 * SLOTS * BLOCK**3, bytes_accessed=6 * MIB, transcendentals=0
        ),
        name="factors",
    )(live, grads, left, right)


def spread(array, axes):
    return lax.all_to_all(array, axes, split_axis=0, concat_axis=0, tiled=True)


def ring(size, step):
    return [(i, (i + step) % size) for i in range(size)]


def gather_row(spot, tokens, grads):
    up, down = ring(N_TENSOR, 1), ring(N_TENSOR, -1)
    ahead, back = ring(X, 1), ring(X, -1)

    cut = cut_tokens(spot, tokens)
    pieces = [cut[0]] + [lax.ppermute(cut[step], "x", ring(X, step)) for step in (1, 3, 2)]
    pieces, grads = lax.optimization_barrier((pieces, grads))
    behind, before = lax.ppermute(grads, "x", ahead), lax.ppermute(grads, "x", back)
    mine = turn(pieces)
    below, above = lax.ppermute(mine, "z", up), lax.ppermute(mine, "z", down)
    whole = [mine, below, above]
    below, above = lax.ppermute(below, "z", up), lax.ppermute(above, "z", down)
    whole += [below, above]
    below, above = lax.ppermute(below, "z", up), lax.ppermute(above, "z", down)
    whole += [below, above]
    behind, before, below, above = lax.optimization_barrier((behind, before, below, above))
    half = grads.shape[-1] // 2
    far = [
        lax.ppermute(behind[..., :half], "x", ahead),
        lax.ppermute(before[..., half:], "x", back),
    ]
    halves = [
        lax.ppermute(below[:LOCAL_ROWS], "z", up),
        lax.ppermute(above[LOCAL_ROWS:], "z", down),
    ]
    return whole + halves, [grads, behind, before], far


def sum_parts(parts):
    mine, other = parts[:Y], lax.ppermute(parts[Y], "core", ring(CORE, 1))
    one, two, three = add_cores(mine, other)
    moved = [
        lax.ppermute(a, "y", ring(Y, step)) for a, step in ((one, 1), (two, 2), (three, 3))
    ]
    return [mine[0], other] + moved


def local(
    tokens, grad_out, owner, left_factor, right_factor,
    left_basis, right_basis, first_moment, second_moment,
):
    owner_row = owner[0]
    block_ids = jnp.arange(NBLK, dtype=jnp.int32)
    same = owner_row[:, None] == owner_row[None, :]
    before = block_ids[None, :] < block_ids[:, None]
    rank = jnp.sum((same & before).astype(jnp.int32), axis=1)
    slot = owner_row * SLOTS + rank
    held = jnp.sum((owner_row == lax.axis_index(DP)).astype(jnp.int32))
    live = (jnp.arange(SLOTS, dtype=jnp.int32) < held).astype(jnp.int32)

    spot = jnp.stack([lax.axis_index(axis) for axis in (*DP, "z")]).astype(jnp.int32)
    grads = grad_out.reshape(N_TENSOR, TOK_SUB, grad_out.shape[1])
    lefts, near, far = gather_row(spot, tokens, grads)
    chunks = [
        sum_parts(gradient_tiles(chunk, spot, lefts, near, far[chunk])) for chunk in range(2)
    ]
    tiles = to_slots(slot, chunks).reshape(N_DP, SLOTS, TILE_ROWS, TILE_COLS)
    update, grad_blocks, first_new, second_new = update_blocks(
        live, spread(tiles, DP), left_basis, right_basis, first_moment, second_moment
    )
    left_new, right_new = update_factors(live, grad_blocks, left_factor, right_factor)
    back = spread(update, DP).reshape(N_DP * SLOTS, TILE_ROWS, TILE_COLS)
    picked = from_slots(slot, back).reshape(N_DP, HOME, TILE_ROWS, TILE_COLS)
    home_update = assemble(spread(picked, DP))
    return (home_update, left_new, right_new, first_new, second_new)


def solution(mesh):
    split = Mesh(mesh.devices.reshape(Y, X, CORE, N_TENSOR), ("y", "x", "core", "z"))
    state = P("z", DP, None, None)
    return jax.shard_map(
        local,
        mesh=split,
        in_specs=(P((*DP, "z"), None), P(DP, "z"), P("z", None)) + (state,) * 6,
        out_specs=(state,) * 5,
        check_vma=False,
    )
```

```python
import jax
import jax.numpy as jnp
from jax import lax
from jax.experimental import pallas as pl
from jax.experimental.pallas import tpu as pltpu
from jax.sharding import Mesh
from jax.sharding import PartitionSpec as P

BLOCK = 256
TILE_ROWS = 16
TILE_COLS = 128
Y, X, CORE = 4, 4, 2
N_DP = Y * X * CORE
N_TENSOR = 8
ROW = X * CORE
STRIP = BLOCK // ROW
SLOTS = 5
HOME = 4
NBLK = 128
ROW_BLOCKS = 16
COL_BLOCKS = 8
TOK_SUB = 32
LOCAL_ROWS = ROW_BLOCKS * STRIP
DP = ("y", "x", "core")
CHIP_ROWS = LOCAL_ROWS * CORE
SHARD_K = X * TOK_SUB
WIDE = 2
CHUNK_K = NBLK // 2

factor_decay = 0.9
first_decay = 0.95
second_decay = 0.95
epsilon_value = 1e-08

MIB = 1024 * 1024
SMEM = pl.BlockSpec(memory_space=pltpu.SMEM)
VMEM = pl.BlockSpec(memory_space=pltpu.VMEM)


def params(mib):
    return pltpu.CompilerParams(vmem_limit_bytes=mib * MIB)


def tile_of(m):
    y, strip = m // ROW, m % ROW
    top, side = STRIP * strip + TILE_ROWS * (y // 2), TILE_COLS * (y % 2)
    return slice(top, top + TILE_ROWS), slice(side, side + TILE_COLS)


def cut_kernel(spot, tokens, *refs):
    outs, (held, pieces, sem) = refs[:X], refs[X:]
    copy = pltpu.make_async_copy(tokens, held, sem)
    copy.start()
    copy.wait()
    for strip in range(ROW):
        pieces[strip // CORE, strip % CORE] = jnp.concatenate(
            [
                held[:, r * BLOCK + STRIP * strip : r * BLOCK + STRIP * (strip + 1)]
                for r in range(ROW_BLOCKS)
            ],
            axis=1,
        )
    for step in range(X):
        chip = (spot[1] + step) % X
        for i in range(CORE):
            core = (spot[2] + i) % CORE
            outs[step][:, i * LOCAL_ROWS : (i + 1) * LOCAL_ROWS] = pieces[chip, core]


def cut_tokens(spot, tokens):
    return pl.pallas_call(
        cut_kernel,
        in_specs=[SMEM, pl.BlockSpec(memory_space=pl.ANY)],
        out_shape=[jax.ShapeDtypeStruct((TOK_SUB, CHIP_ROWS), jnp.bfloat16)] * X,
        scratch_shapes=[
            pltpu.VMEM(tokens.shape, jnp.bfloat16),
            pltpu.VMEM((X, CORE, TOK_SUB, LOCAL_ROWS), jnp.bfloat16),
            pltpu.SemaphoreType.DMA(()),
        ],
        compiler_params=params(16),
        name="cut_tokens",
    )(spot, tokens)


def turn_kernel(*refs):
    out = refs[X]
    out[...] = jnp.concatenate([piece[...] for piece in refs[:X]], axis=0).T


def turn(pieces):
    return pl.pallas_call(
        turn_kernel,
        out_shape=jax.ShapeDtypeStruct((CHIP_ROWS, SHARD_K), jnp.bfloat16),
        compiler_params=params(16),
        name="turn",
    )(*pieces)


def gradient_kernel(spot, *refs):
    whole, halves, sources = refs[:7], refs[7:9], refs[9:13]
    mine, other, (left, right, tiles) = refs[13:17], refs[17], refs[18:]

    @pl.when(pl.program_id(0) == 0)
    def join_tokens():
        for j in range(7):
            left[:, j * SHARD_K : (j + 1) * SHARD_K] = whole[j][...]
        left[:LOCAL_ROWS, 7 * SHARD_K :] = halves[0][...]
        left[LOCAL_ROWS:, 7 * SHARD_K :] = halves[1][...]

    for j, step in enumerate((0, -1, 1, -2, 2, -3, 3, 4)):
        place = (spot[3] + step + N_TENSOR) % N_TENSOR
        for i in range(X):
            top = j * SHARD_K + i * TOK_SUB
            right[top : top + TOK_SUB] = sources[i][place]
    for column in range(WIDE):
        result = jnp.dot(
            left[...], right[:, column * BLOCK : (column + 1) * BLOCK],
            preferred_element_type=jnp.float32,
        ).astype(jnp.bfloat16)
        for side in range(CORE):
            for r in range(ROW_BLOCKS):
                for y in range(Y):
                    rows, cols = tile_of(y * ROW)
                    top = side * LOCAL_ROWS + r * STRIP + rows.start
                    tiles[side, y, column * ROW_BLOCKS + r] = result[top : top + TILE_ROWS, cols]
    for step in range(Y):
        place = (spot[0] + step) % Y
        mine[step][...] = tiles[0, place]
        other[step] = tiles[1, place]


def gradient_tiles(chunk, spot, lefts, near, far):
    resident = lambda a: pl.BlockSpec(a.shape, lambda c, spot: (0, 0))
    steps = COL_BLOCKS // 2 // WIDE
    blocks = WIDE * ROW_BLOCKS
    shape = (N_TENSOR, TOK_SUB, WIDE * BLOCK)
    near_spec = pl.BlockSpec(shape, lambda c, spot: (0, 0, steps * chunk + c))
    far_spec = pl.BlockSpec(shape, lambda c, spot: (0, 0, c))
    part = pl.BlockSpec((blocks, TILE_ROWS, TILE_COLS), lambda c, spot: (c, 0, 0))
    return pl.pallas_call(
        gradient_kernel,
        grid_spec=pltpu.PrefetchScalarGridSpec(
            num_scalar_prefetch=1,
            grid=(steps,),
            in_specs=[resident(a) for a in lefts] + [near_spec] * 3 + [far_spec],
            out_specs=[part] * Y
            + [pl.BlockSpec((Y, blocks, TILE_ROWS, TILE_COLS), lambda c, spot: (0, c, 0, 0))],
            scratch_shapes=[
                pltpu.VMEM((CHIP_ROWS, N_TENSOR * SHARD_K), jnp.bfloat16),
                pltpu.VMEM((N_TENSOR * SHARD_K, WIDE * BLOCK), jnp.bfloat16),
                pltpu.VMEM((CORE, Y, blocks, TILE_ROWS, TILE_COLS), jnp.bfloat16),
            ],
        ),
        out_shape=[jax.ShapeDtypeStruct((CHUNK_K, TILE_ROWS, TILE_COLS), jnp.bfloat16)] * Y
        + [jax.ShapeDtypeStruct((Y, CHUNK_K, TILE_ROWS, TILE_COLS), jnp.bfloat16)],
        compiler_params=params(30),
        cost_estimate=pl.CostEstimate(
            flops=2 * CHIP_ROWS * N_TENSOR * SHARD_K * 4 * BLOCK,
            bytes_accessed=8 * MIB, transcendentals=0,
        ),
        name="gradient_tiles",
    )(spot, *lefts, *near, far)


def add_cores_kernel(one, two, three, other, *outs):
    for d, (mine, out) in enumerate(zip((one, two, three), outs), 1):
        out[...] = (mine[...].astype(jnp.float32) + other[d].astype(jnp.float32)).astype(
            jnp.bfloat16
        )


def add_cores(parts, other):
    return pl.pallas_call(
        add_cores_kernel,
        out_shape=[jax.ShapeDtypeStruct(a.shape, a.dtype) for a in parts[1:]],
        compiler_params=params(16),
        name="add_cores",
    )(*parts[1:], other)


def sum_kernel(mine, other, one, two, three, out):
    total = mine[...].astype(jnp.float32) + other[0].astype(jnp.float32)
    for part in (one, two, three):
        total = total + part[...].astype(jnp.float32)
    out[...] = total.astype(jnp.bfloat16)


def sum_chunk(parts):
    return pl.pallas_call(
        sum_kernel,
        out_shape=jax.ShapeDtypeStruct((CHUNK_K, TILE_ROWS, TILE_COLS), jnp.bfloat16),
        compiler_params=params(16),
        cost_estimate=pl.CostEstimate(flops=MIB, bytes_accessed=2 * MIB, transcendentals=0),
        name="sum_chunk",
    )(*parts)


def to_slots_kernel(slot, summed, mine, other, one, two, three, out):
    out[...] = jnp.zeros_like(out)

    def early(k, carry):
        out[slot[k]] = summed[k]
        return carry

    def late(k, carry):
        total = mine[k].astype(jnp.float32) + other[0, k].astype(jnp.float32)
        for part in (one, two, three):
            total = total + part[k].astype(jnp.float32)
        out[slot[CHUNK_K + k]] = total.astype(jnp.bfloat16)
        return carry

    lax.fori_loop(0, CHUNK_K, early, 0, unroll=16)
    lax.fori_loop(0, CHUNK_K, late, 0, unroll=16)


def to_slots(slot, chunks):
    return pl.pallas_call(
        to_slots_kernel,
        in_specs=[SMEM] + [VMEM] * 6,
        out_shape=jax.ShapeDtypeStruct((N_DP * SLOTS, TILE_ROWS, TILE_COLS), jnp.bfloat16),
        compiler_params=params(16),
        name="to_slots",
    )(slot, sum_chunk(chunks[0]), *chunks[1])


def from_slots_kernel(slot, tiles, out):
    def body(k, carry):
        out[k] = tiles[slot[k]]
        return carry

    lax.fori_loop(0, NBLK, body, 0, unroll=32)


def from_slots(slot, tiles):
    return pl.pallas_call(
        from_slots_kernel,
        in_specs=[SMEM, VMEM],
        out_shape=jax.ShapeDtypeStruct((NBLK, TILE_ROWS, TILE_COLS), jnp.bfloat16),
        compiler_params=params(16),
        name="from_slots",
    )(slot, tiles)


def assemble_kernel(tiles, out):
    for h in range(HOME):
        for m in range(N_DP):
            rows, cols = tile_of(m)
            out[0, h, rows, cols] = tiles[m, h]


def assemble(tiles):
    return pl.pallas_call(
        assemble_kernel,
        out_shape=jax.ShapeDtypeStruct((1, HOME, BLOCK, BLOCK), jnp.bfloat16),
        compiler_params=params(16),
        name="assemble",
    )(tiles)


def dot(a, b, ca, cb):
    return lax.dot_general(a, b, (((ca,), (cb,)), ((), ())), preferred_element_type=jnp.float32)


def update_kernel(
    live, tiles, basis_left, basis_right, first, second,
    update, grads, first_new, second_new,
):
    for s in range(SLOTS):
        for m in range(N_DP):
            rows, cols = tile_of(m)
            grads[s, rows, cols] = tiles[m, s]
        grad = grads[s]
        ql, qr = basis_left[0, s], basis_right[0, s]
        halfway = dot(ql, grad, 0, 0).astype(jnp.bfloat16)
        rotated = dot(halfway, qr, 1, 0)
        first_old, second_old = first[0, s], second[0, s]
        first_float = first_decay * first_old.astype(jnp.float32) + (1.0 - first_decay) * rotated
        second_float = (
            second_decay * second_old.astype(jnp.float32)
            + (1.0 - second_decay) * rotated * rotated
        )
        ratio = (first_float / (jnp.sqrt(second_float) + epsilon_value)).astype(jnp.bfloat16)
        turned = dot(ql, ratio, 1, 0).astype(jnp.bfloat16)
        result = dot(turned, qr, 1, 1).astype(jnp.bfloat16)
        for m in range(N_DP):
            rows, cols = tile_of(m)
            update[m, s] = result[rows, cols]
        alive = live[s] > 0
        first_new[0, s] = jnp.where(alive, first_float.astype(jnp.bfloat16), first_old)
        second_new[0, s] = jnp.where(alive, second_float.astype(jnp.bfloat16), second_old)


def update_blocks(live, tiles, basis_left, basis_right, first, second):
    like = lambda a: jax.ShapeDtypeStruct(a.shape, a.dtype)
    return pl.pallas_call(
        update_kernel,
        in_specs=[SMEM] + [VMEM] * 5,
        out_shape=[
            like(tiles),
            jax.ShapeDtypeStruct((SLOTS, BLOCK, BLOCK), jnp.bfloat16),
            like(first),
            like(second),
        ],
        compiler_params=params(48),
        name="update",
    )(live, tiles, basis_left, basis_right, first, second)


def factor_kernel(live, grads, left, right, left_new, right_new):
    alive = live[pl.program_id(0)] > 0
    grad = grads[0]
    scale = (1.0 - factor_decay) / BLOCK
    left_old, right_old = left[0, 0], right[0, 0]
    left_new[0, 0] = jnp.where(
        alive, factor_decay * left_old + scale * dot(grad, grad, 1, 1), left_old
    )
    right_new[0, 0] = jnp.where(
        alive, factor_decay * right_old + scale * dot(grad, grad, 0, 0), right_old
    )


def update_factors(live, grads, left, right):
    state = pl.BlockSpec((1, 1, BLOCK, BLOCK), lambda s, live: (0, s, 0, 0))
    return pl.pallas_call(
        factor_kernel,
        grid_spec=pltpu.PrefetchScalarGridSpec(
            num_scalar_prefetch=1,
            grid=(SLOTS,),
            in_specs=[pl.BlockSpec((1, BLOCK, BLOCK), lambda s, live: (s, 0, 0))] + [state] * 2,
            out_specs=[state] * 2,
        ),
        out_shape=[jax.ShapeDtypeStruct(a.shape, a.dtype) for a in (left, right)],
        compiler_params=params(32),
        cost_estimate=pl.CostEstimate(
            flops=4 * SLOTS * BLOCK**3, bytes_accessed=6 * MIB, transcendentals=0
        ),
        name="factors",
    )(live, grads, left, right)


def spread(array, axes):
    return lax.all_to_all(array, axes, split_axis=0, concat_axis=0, tiled=True)


def ring(size, step):
    return [(i, (i + step) % size) for i in range(size)]


def gather_row(spot, tokens, grads):
    up, down = ring(N_TENSOR, 1), ring(N_TENSOR, -1)
    ahead, back = ring(X, 1), ring(X, -1)

    cut = cut_tokens(spot, tokens)
    pieces = [cut[0]] + [lax.ppermute(cut[step], "x", ring(X, step)) for step in (1, 3, 2)]
    pieces, grads = lax.optimization_barrier((pieces, grads))
    behind, before = lax.ppermute(grads, "x", ahead), lax.ppermute(grads, "x", back)
    mine = turn(pieces)
    below, above = lax.ppermute(mine, "z", up), lax.ppermute(mine, "z", down)
    whole = [mine, below, above]
    below, above = lax.ppermute(below, "z", up), lax.ppermute(above, "z", down)
    whole += [below, above]
    below, above = lax.ppermute(below, "z", up), lax.ppermute(above, "z", down)
    whole += [below, above]
    behind, before, below, above = lax.optimization_barrier((behind, before, below, above))
    half = grads.shape[-1] // 2
    far = [
        lax.ppermute(behind[..., :half], "x", ahead),
        lax.ppermute(before[..., half:], "x", back),
    ]
    halves = [
        lax.ppermute(below[:LOCAL_ROWS], "z", up),
        lax.ppermute(above[LOCAL_ROWS:], "z", down),
    ]
    return whole + halves, [grads, behind, before], far


def sum_parts(parts):
    mine, other = parts[:Y], lax.ppermute(parts[Y], "core", ring(CORE, 1))
    one, two, three = add_cores(mine, other)
    moved = [
        lax.ppermute(a, "y", ring(Y, step)) for a, step in ((one, 1), (two, 2), (three, 3))
    ]
    return [mine[0], other] + moved


def local(
    tokens, grad_out, owner, left_factor, right_factor,
    left_basis, right_basis, first_moment, second_moment,
):
    owner_row = owner[0]
    block_ids = jnp.arange(NBLK, dtype=jnp.int32)
    same = owner_row[:, None] == owner_row[None, :]
    before = block_ids[None, :] < block_ids[:, None]
    rank = jnp.sum((same & before).astype(jnp.int32), axis=1)
    slot = owner_row * SLOTS + rank
    held = jnp.sum((owner_row == lax.axis_index(DP)).astype(jnp.int32))
    live = (jnp.arange(SLOTS, dtype=jnp.int32) < held).astype(jnp.int32)
    slot, live = lax.optimization_barrier((slot, live))

    spot = jnp.stack([lax.axis_index(axis) for axis in (*DP, "z")]).astype(jnp.int32)
    grads = grad_out.reshape(N_TENSOR, TOK_SUB, grad_out.shape[1])
    lefts, near, far = gather_row(spot, tokens, grads)
    chunks = [
        sum_parts(gradient_tiles(chunk, spot, lefts, near, far[chunk])) for chunk in range(2)
    ]
    tiles = to_slots(slot, chunks).reshape(N_DP, SLOTS, TILE_ROWS, TILE_COLS)
    update, grad_blocks, first_new, second_new = update_blocks(
        live, spread(tiles, DP), left_basis, right_basis, first_moment, second_moment
    )
    left_new, right_new = update_factors(live, grad_blocks, left_factor, right_factor)
    back = spread(update, DP).reshape(N_DP * SLOTS, TILE_ROWS, TILE_COLS)
    picked = from_slots(slot, back).reshape(N_DP, HOME, TILE_ROWS, TILE_COLS)
    home_update = assemble(spread(picked, DP))
    return (home_update, left_new, right_new, first_new, second_new)


def solution(mesh):
    split = Mesh(mesh.devices.reshape(Y, X, CORE, N_TENSOR), ("y", "x", "core", "z"))
    state = P("z", DP, None, None)
    return jax.shard_map(
        local,
        mesh=split,
        in_specs=(P((*DP, "z"), None), P(DP, "z"), P("z", None)) + (state,) * 6,
        out_specs=(state,) * 5,
        check_vma=False,
    )
```
